32 devices in a mesh: grp: 2 (over y), col: 4 (over z), lev: 4 (over x, core).
Axes of the slice: x: 2, y: 2, z: 4, core: 2. Of those that a mesh axis runs over, the one named last changes fastest.
Arguments:
- control: float32 [256, 32, 256], P(('grp', 'lev'), 'col'), parts along dimension 0, may hold values from -6 to 6
- control_ens: float32 [4, 128, 32, 256], P('grp', 'lev', 'col'), parts along dimension 0, may hold values from -6 to 6
- ensemble: bfloat16 [4, 128, 32, 256], P('grp', 'lev', 'col'), parts along dimension 0, may hold values from -6 to 6
- spread: float32 [256, 32, 256], P(('grp', 'lev'), 'col'), parts along dimension 0, may hold values from 0.3 to 3
- jacobian: bfloat16 [128, 128, 128], P(('grp', 'col'), 'lev'), parts along dimension 0, may hold values from -0.5 to 0.5
- obs_value: bfloat16 [128, 128], P(('grp', 'col')), parts along dimension 0, may hold values from -6 to 6
- obs_weight: bfloat16 [128, 128], P(('grp', 'col')), parts along dimension 0, may hold values from 1 to 10
- channel_mask: int32 [128, 128], P(('grp', 'col')), parts along dimension 0, may hold values 0 or 1
- obs_cell: int32 [128], P(('grp', 'col')), parts along dimension 0, may hold values from 0 to 2047
- obs_count: int32 [8, 4], P(('grp', 'col')), parts along dimension 0, may hold values from 1 to 4, as said below
Outputs:
- grad_control: float32 [256, 32, 256], P(('grp', 'lev'), 'col'), parts along dimension 0
- grad_ens: float32 [4, 128, 32, 256], P('grp', 'lev', 'col'), parts along dimension 0
- departures: float32 [128, 128], P(('grp', 'col')), parts along dimension 0
The draws below stay inside these ranges and needn't reach their ends.
There are 2 independent parts, one for each index of `grp`. The reference program is written for one: setup_inputs(seed, part) draws one part's arguments, and reference() takes and returns one part's arrays. A program takes and returns all parts, laid end to end along the dimension named above; each array names one. Nothing has to cross between parts.
Inputs may be any that keep to these rules, and one draw needn't show every extreme that they name: `obs_count`: for every sending block some target gets exactly 4 filled slots, and one target gets 4 from every sending block.
All inputs are finite; a program needn't handle non-finite values. No bound on the sum of `channel_mask` on one device may be relied on, other than what follows from the above.
Results may differ from the reference program's by a relative error of at most 0.0013.
Values may be sent and summed in bfloat16 or wider, within the bound.
A program may use at most 64 MiB of HBM per device.

```python
import math
import jax
import jax.numpy as jnp
from jax import lax

LEV = 128
CHAN = 128
CX = 8
NY = 256
CAP = 4
E = 2
STEPS = 4
NX = 32
ROWS = 64
N_COL = 4


def draw_obs_count(key, part):
    key = jax.random.fold_in(key, 11)
    key_base, key_hot = jax.random.split(key, 2)
    counts = jax.random.randint(key_base, (N_COL, N_COL), 1, CAP + 1)
    hot_target = jax.random.randint(key_hot, (), 0, N_COL)
    counts = jnp.where(jnp.arange(N_COL)[None, :] == hot_target, CAP, counts)
    return counts.astype(jnp.int32)


def touch_ends(values, key, smallest, largest):
    longest = values.shape.index(max(values.shape))
    spots = []
    for shift in (0, 1):
        where = [jax.random.randint(jax.random.fold_in(key, axis), (), 0, length) for axis, length in enumerate(values.shape)]
        where[longest] = (where[longest] + shift) % values.shape[longest]
        spots.append(tuple(where))
    return values.at[spots[0]].set(smallest).at[spots[1]].set(largest)


def block_levels(own_key, shape, shards, low, largest):
    loudness, own = 1.0, jax.random.fold_in(own_key, 6)
    for axis_at, shards_of in shards:
        heights = jnp.exp(jax.random.uniform(jax.random.fold_in(own, axis_at), (shards_of,), jnp.float32, low / len(shards), largest / len(shards)))
        loudness = loudness * jnp.repeat(heights, shape[axis_at] // shards_of).reshape([-1 if axis == axis_at else 1 for axis in range(len(shape))])
    return loudness


def centred(rng, extent, scale, bound, cuts=(), held_as=jnp.bfloat16):
    factor_of = block_levels(rng, extent, cuts, -0.22, 0.18) if cuts else 1.0
    drawn = jax.random.normal(rng, extent, jnp.float32) * scale * factor_of
    return jnp.minimum(jnp.maximum(drawn, -bound), bound).astype(held_as)


def setup_inputs(seed: int = 0, part: int = 0) -> dict:
    streams_of = jax.random.split(jax.random.key(seed), 11)
    part_keys = jax.random.split(jax.random.fold_in(streams_of[10], part), 11)
    return {
        "control": centred(part_keys[0], (LEV, NX, NY), 1.0, 6.0, ((0, 4), (1, 4)), jnp.float32),
        "control_ens": centred(part_keys[1], (E, LEV, NX, NY), 1.0, 6.0, ((1, 4), (2, 4)), jnp.float32),
        "ensemble": centred(part_keys[2], (E, LEV, NX, NY), 1.0, 6.0, ((1, 4), (2, 4))),
        "spread": jnp.clip(jnp.exp(math.log(3.0) - 2.3025851 * jax.random.uniform(part_keys[3], (LEV, NX, NY), jnp.float32) ** block_levels(part_keys[3], (LEV, NX, NY), ((0, 4), (1, 4)), -0.2, 0.2)), 0.3, 3.0),
        "jacobian": centred(part_keys[4], (ROWS, LEV, CHAN), LEV ** -0.5, 0.5, ((0, 4), (1, 4))),
        "obs_value": centred(part_keys[5], (ROWS, CHAN), 1.0, 6.0, ((0, 4),)),
        "obs_weight": jnp.clip(jnp.exp(math.log(10.0) - 2.3025851 * jax.random.uniform(part_keys[6], (ROWS, CHAN), jnp.float32) ** block_levels(part_keys[6], (ROWS, CHAN), ((0, 4),), -0.2, 0.2)), 1.0, 10.0).astype(jnp.bfloat16),
        "channel_mask": touch_ends((jax.random.randint(part_keys[7], (ROWS, CHAN), 0, 4) < 3).astype(jnp.int32), jax.random.fold_in(part_keys[7], 1), 0, 1),
        "obs_cell": touch_ends(jax.random.randint(part_keys[8], (ROWS,), 0, CX * NY), jax.random.fold_in(part_keys[8], 1), 0, (CX * NY) - 1).astype(jnp.int32),
        "obs_count": draw_obs_count(jax.random.fold_in(jax.random.fold_in(streams_of[10], part), 71), part),
    }


rate_x = 0.35
rate_y = 0.1

def smooth(fields):
    for iteration in range(STEPS):
        padded = jnp.pad(fields, ((0, 0), (0, 0), (0, 0), (1, 1)))
        along_x = jnp.roll(fields, 1, 2) + jnp.roll(fields, -1, 2) - 2.0 * fields
        along_y = padded[..., 2:] + padded[..., :-2] - 2.0 * fields
        fields = fields + rate_x * along_x + rate_y * along_y
    return fields

def reference(control, control_ens, ensemble, spread, jacobian, obs_value, obs_weight, channel_mask, obs_cell, obs_count):
    ens_scale = 1.0 / math.sqrt(E)
    ens_float = ensemble.astype(jnp.float32)
    smoothed = smooth(jnp.concatenate([control[None], control_ens], 0))
    analysis = spread * smoothed[0] + lax.optimization_barrier(jnp.sum(ens_float * smoothed[1:], 0)) * ens_scale
    flat_state = analysis.reshape(LEV, NX * NY)
    row_ids = jnp.arange(ROWS, dtype=jnp.int32)
    target = row_ids // CAP % N_COL
    source = row_ids // (N_COL * CAP)
    slot_index = row_ids % CAP
    flat_index = (target * (CX * NY) + obs_cell).astype(jnp.int32)
    filled = slot_index < obs_count[source, target]
    columns = flat_state[:, flat_index].T.astype(jnp.bfloat16)
    jac_blocks = jacobian.reshape(N_COL, N_COL * CAP, LEV, CHAN)

    def forward(pair):
        return jnp.einsum('rlc,rl->rc', pair[0].astype(jnp.float32), pair[1].astype(jnp.float32))
    radiance = lax.map(forward, (jac_blocks, columns.reshape(N_COL, N_COL * CAP, LEV))).reshape(ROWS, CHAN)
    active = filled[:, None] & (channel_mask > 0)
    departures = jnp.where(active, obs_weight.astype(jnp.float32) * (radiance - obs_value.astype(jnp.float32)), 0.0)
    dep_rounded = departures.astype(jnp.bfloat16)

    def backward(pair):
        return jnp.einsum('rc,rlc->rl', pair[0].astype(jnp.float32), pair[1].astype(jnp.float32))
    increments = lax.map(backward, (dep_rounded.reshape(N_COL, N_COL * CAP, CHAN), jac_blocks)).reshape(ROWS, LEV)
    gradient_flat = jnp.zeros((LEV, NX * NY), jnp.float32).at[:, flat_index].add(increments.T)
    gradient_field = gradient_flat.reshape(LEV, NX, NY)
    adjoint = smooth(jnp.concatenate([(spread * gradient_field)[None], ens_float * gradient_field[None] * ens_scale], 0))
    return (control + adjoint[0], control_ens + adjoint[1:], departures)
```

```python
import math

import jax
import jax.numpy as jnp
from jax import lax
from jax.experimental import pallas as pl
from jax.experimental.pallas import tpu as pltpu
from jax.sharding import PartitionSpec as P
import functools
import numpy as np

STEPS = 4


rate_x = 0.35
rate_y = 0.1


def padded_2(value, sides, width):
    for axis, dim in sides:
        peers, length = (lax.axis_size(axis), value.shape[dim])
        up = [(i, (i + 1) % peers) for i in range(peers)]
        down = [(j, i) for i, j in up]
        last = lax.slice_in_dim(value, length - width, length, axis=dim)
        initial = lax.slice_in_dim(value, 0, width, axis=dim)
        before = lax.ppermute(last, axis, up)
        after = lax.ppermute(initial, axis, down)
        value = jnp.concatenate([before, value, after], axis=dim)
    return value


def smooth(fields):
    for iteration in range(STEPS):
        padded = padded_2(fields, (("col", 2),), 1)
        beside = jnp.pad(fields, ((0, 0), (0, 0), (0, 0), (1, 1)))
        along_x = padded[:, :, 2:, :] + padded[:, :, :-2, :] - 2.0 * fields
        along_y = beside[..., 2:] + beside[..., :-2] - 2.0 * fields
        fields = fields + rate_x * along_x + rate_y * along_y
    return fields


def solve_rows(jac_rows, columns, values, weights, masks, filled):
    partial_value = jnp.einsum("rlc,rl->rc", jac_rows, columns, preferred_element_type=jnp.float32)
    radiance = lax.psum(partial_value, "lev")
    active = (filled[:, None] > 0) & (masks > 0)
    departure = jnp.where(
        active, weights.astype(jnp.float32) * (radiance - values.astype(jnp.float32)), 0.0
    )
    increment = jnp.einsum(
        "rc,rlc->rl", departure.astype(jnp.bfloat16), jac_rows, preferred_element_type=jnp.float32
    )
    return (departure, increment)


def local(
    control,
    control_ens,
    ensemble,
    spread,
    jacobian,
    obs_value,
    obs_weight,
    channel_mask,
    obs_cell,
    obs_count,
):
    members = control_ens.shape[0]
    ens_scale = 1.0 / math.sqrt(members)
    levels, cells_x, cells_y = control.shape
    peer_count = lax.axis_size("col")
    slot_total = jacobian.shape[0]
    capacity = slot_total // peer_count
    smoothed = smooth(jnp.concatenate([control[None], control_ens], 0))
    analysis = spread * smoothed[0] + jnp.sum(ensemble * smoothed[1:], 0) * ens_scale
    flat_state = analysis.reshape(levels, cells_x * cells_y)
    row_ids = jnp.arange(slot_total, dtype=jnp.int32)
    target = row_ids // capacity
    slot_index = row_ids % capacity
    filled = (slot_index < obs_count[0][target]).astype(jnp.int32)
    empty_grid = jnp.zeros((levels, cells_x * cells_y), jnp.float32)
    jac_recv, value_recv, weight_recv, mask_recv, cell_recv, filled_recv = (
        lax.all_to_all(jacobian, "col", split_axis=0, concat_axis=0, tiled=True),
        lax.all_to_all(obs_value, "col", split_axis=0, concat_axis=0, tiled=True),
        lax.all_to_all(obs_weight, "col", split_axis=0, concat_axis=0, tiled=True),
        lax.all_to_all(channel_mask, "col", split_axis=0, concat_axis=0, tiled=True),
        lax.all_to_all(obs_cell, "col", split_axis=0, concat_axis=0, tiled=True),
        lax.all_to_all(filled, "col", split_axis=0, concat_axis=0, tiled=True),
    )
    columns = flat_state[:, cell_recv].T.astype(jnp.bfloat16)
    departure, increment = solve_rows(
        jac_recv, columns, value_recv, weight_recv, mask_recv, filled_recv
    )
    gradient_flat = empty_grid.at[:, cell_recv].add(increment.T)
    departures = lax.all_to_all(departure, "col", split_axis=0, concat_axis=0, tiled=True)
    gradient_field = gradient_flat.reshape(levels, cells_x, cells_y)
    adjoint = smooth(
        jnp.concatenate(
            [(spread * gradient_field)[None], ensemble * gradient_field[None] * ens_scale], 0
        )
    )
    return (control + adjoint[0], control_ens + adjoint[1:], departures)


LANES = 128


def stencil_power():
    step = np.array([[0.0, rate_x, 0.0], [rate_y, 1.0 - 2.0 * rate_x - 2.0 * rate_y, rate_y], [0.0, rate_x, 0.0]])
    total = np.zeros((2 * STEPS + 1, 2 * STEPS + 1))
    total[STEPS, STEPS] = 1.0
    for _ in range(STEPS):
        wide = np.pad(total, 1)
        total = sum(
            step[i, j] * wide[i : i + 2 * STEPS + 1, j : j + 2 * STEPS + 1]
            for i in range(3)
            for j in range(3)
        )
    return total[STEPS:, STEPS:]


def split(value):
    high = value.astype(jnp.bfloat16)
    return high, (value - high.astype(jnp.float32)).astype(jnp.bfloat16)


def dot(a, b, b_dim):
    return lax.dot_general(a, b, (((1,), (b_dim,)), ((), ())), preferred_element_type=jnp.float32)


def spread_groups(value, width):
    total = value
    for shift in range(width, LANES, width):
        total = total + pltpu.roll(value, shift, 1)
    return total


def fused(
    cfg,
    ctl_hbm, cen_hbm, ens_hbm, spr_hbm, jac_hbm, val_ref, wgt_ref, msk_ref, cell_ref, count_ref,
    octl_hbm, ocen_hbm, dep_ref,
    ctl, cen, ens, ensf, spr, jac, cells, ey, fst, vst, wst, pv, pv_in, rad_in, a_all,
    in_sem, out_sem, send_sem, recv_sem,
):
    cols, levs, slots, lev, cx, ny = cfg
    cap = slots // cols
    nx = cols * cx
    every = cols * slots
    me, my_lev = lax.axis_index("col"), lax.axis_index("lev")
    table = stencil_power()

    halves = range(ny // LANES)
    lanes_of = [slice(h * LANES, (h + 1) * LANES) for h in halves]
    pairs = [(ctl_hbm.at[:, lanes_of[h]], ctl.at[h]) for h in halves]
    pairs += [(cen_hbm.at[e, :, lanes_of[h]], cen.at[e, h]) for e in range(2) for h in halves]
    fields = len(pairs)
    pairs += [(ens_hbm, ens)] + [(spr_hbm.at[:, lanes_of[h]], spr.at[h]) for h in halves]
    pairs += [(jac_hbm, jac)]
    loads = [pltpu.make_async_copy(src, dst, in_sem.at[i]) for i, (src, dst) in enumerate(pairs)]
    for load in loads:
        load.start()

    barrier = pltpu.get_barrier_semaphore()
    for d in range(1, cols):
        pl.semaphore_signal(
            barrier, inc=1, device_id={"col": lax.rem(me + d, cols)}, device_id_type=pl.DeviceIdType.MESH
        )
    for d in range(1, levs):
        pl.semaphore_signal(
            barrier, inc=1, device_id={"lev": lax.rem(my_lev + d, levs)}, device_id_type=pl.DeviceIdType.MESH
        )

    def send(phase, axis, peers, mine, src_of, dst):
        copies = []
        for d in range(1, peers):
            to = lax.rem(mine + d, peers)
            copy = pltpu.make_async_remote_copy(
                src_ref=src_of(to),
                dst_ref=dst,
                send_sem=send_sem.at[phase, d],
                recv_sem=recv_sem.at[phase, d],
                device_id={axis: to},
                device_id_type=pl.DeviceIdType.MESH,
            )
            copy.start()
            copies.append(copy)
        return copies

    row = lax.broadcasted_iota(jnp.int32, (slots, LANES), 0)
    lane = lax.broadcasted_iota(jnp.int32, (slots, LANES), 1)
    own = jnp.zeros((slots, LANES), jnp.int32)
    for r in range(slots):
        own = jnp.where(row == r, cell_ref[r], own)
    my_rows = pl.ds(pl.multiple_of(me * slots, slots), slots)
    cells[my_rows, :] = own
    pl.semaphore_wait(barrier, cols + levs - 2)
    cell_copies = send(0, "col", cols, me, lambda to: cells.at[my_rows], cells.at[my_rows])

    for load in loads[:fields]:
        load.wait()
    zeros = jnp.zeros((lev, ny), jnp.bfloat16)
    picks = [pl.ds(x, lev, stride=cx) for x in range(cx)]
    for x in range(cx):
        for i, ref in enumerate((ctl, cen.at[0], cen.at[1])):
            for h in halves:
                high, low = split(ref.at[h][picks[x], :])
                fst[x, i * lev : (i + 1) * lev, lanes_of[h]] = high
                fst[x, LANES + i * lev : LANES + (i + 1) * lev, lanes_of[h]] = low
        fst[x, 3 * lev : 4 * lev, :] = zeros
        fst[x, LANES + 3 * lev : LANES + 4 * lev, :] = zeros
    for load in loads[fields:-1]:
        load.wait()
    for e in range(2):
        member = ens[e].astype(jnp.float32).reshape(lev * cx, ny)
        for h in halves:
            ensf[e, h] = member[:, lanes_of[h]]
    for x in range(cx):
        for h in halves:
            high, low = split(spr.at[h][picks[x], :])
            vst[x, 0:lev, lanes_of[h]] = high
            vst[x, lev : 2 * lev, lanes_of[h]] = ensf.at[0, h][picks[x], :].astype(jnp.bfloat16)
            vst[x, 2 * lev : 3 * lev, lanes_of[h]] = ensf.at[1, h][picks[x], :].astype(jnp.bfloat16)
            vst[x, 3 * lev : 4 * lev, lanes_of[h]] = low

    for copy in cell_copies:
        copy.wait()

    cell = cells[...]
    shift = ny.bit_length() - 1
    cell_x = lax.shift_right_logical(cell, jnp.full_like(cell, shift))
    cell_y = cell & (ny - 1)
    slot = lax.broadcasted_iota(jnp.int32, (every, LANES), 0)
    target = lax.shift_right_logical(slot, jnp.full_like(slot, cap.bit_length() - 1)) & (cols - 1)
    apart = me * cx - (target * cx + cell_x)
    y_lane = lax.broadcasted_iota(jnp.int32, (every, LANES), 1)
    for h in range(ny // LANES):
        y = y_lane + h * LANES
        dy = jnp.abs(y - cell_y)
        below = y + cell_y + 2
        above = 2 * ny - y - cell_y
        for m in range(STEPS + 1):
            one = jnp.where(dy == m, 1.0, 0.0)
            if m >= 2:
                one = one - jnp.where((below == m) | (above == m), 1.0, 0.0)
            ey[m, :, h * LANES : (h + 1) * LANES] = one
    out = None
    for x in range(cx):
        dx = apart + x
        dx = jnp.where(dx >= nx // 2, dx - nx, dx)
        dx = jnp.abs(jnp.where(dx < -(nx // 2), dx + nx, dx))
        at = [dx == q for q in range(STEPS + 1)]
        factors = []
        for m in range(STEPS + 1):
            factor = jnp.zeros((every, LANES), jnp.float32)
            for q in range(STEPS + 1 - m):
                factor = jnp.where(at[q], float(table[q, m]), factor)
            factors.append(factor)
        here = jnp.where(at[0], 1.0, 0.0)
        hits = []
        for h in range(ny // LANES):
            part = slice(h * LANES, (h + 1) * LANES)
            centre = ey[0, :, part]
            weight = factors[0] * centre
            for m in range(1, STEPS + 1):
                weight = weight + factors[m] * ey[m, :, part]
            high, low = split(weight)
            wst[x, 0:every, part] = high
            wst[x, every : 2 * every, part] = low
            wst[x, 2 * every : 3 * every, part] = high
            hits.append((here * centre).astype(jnp.bfloat16))
        sums = dot(wst[x, 0 : 2 * every, :], fst[x], 1)
        found = dot(jnp.concatenate(hits, axis=1), vst[x], 1)
        out = (sums, found) if out is None else (out[0] + sums, out[1] + found)
    sums, found = out
    pv[:, 0:LANES] = sums[0:every, 0:LANES] + sums[0:every, LANES:] + sums[every:, 0:LANES]
    group = lax.shift_right_logical(y_lane, jnp.full_like(y_lane, lev.bit_length() - 1))
    found = jnp.where(group == 0, found + pltpu.roll(found, lev, 1), found * (1.0 / math.sqrt(2)))
    pv[:, LANES:] = jnp.where(group == 3, 0.0, found)
    pv_in[me] = pv[my_rows, :]
    copies = send(
        1, "col", cols, me,
        lambda to: pv.at[pl.ds(pl.multiple_of(to * slots, slots), slots)], pv_in.at[me],
    )
    loads[-1].wait()
    for copy in copies:
        copy.wait()

    both = pv_in[0]
    for s in range(1, cols):
        both = both + pv_in[s]
    values = both[:, LANES:]
    columns = spread_groups(both[:, 0:LANES] * values, lev)
    jac_rows = jac[...].reshape(slots * lev, LANES)
    per = LANES // lev
    lane_group = lax.shift_right_logical(lane, jnp.full_like(lane, lev.bit_length() - 1))
    tiles = slots // per
    block = jnp.concatenate(
        [jnp.where(row == q * per + lane_group, columns, 0.0) for q in range(tiles)], axis=1
    ).astype(jnp.bfloat16)
    rad_in[my_lev] = dot(block, jac_rows, 0)
    for copy in send(2, "lev", levs, my_lev, lambda to: rad_in.at[my_lev], rad_in.at[my_lev]):
        copy.wait()
    radiance = rad_in[0]
    for s in range(1, levs):
        radiance = radiance + rad_in[s]

    filled = jnp.zeros((slots, LANES), jnp.bool_)
    for t in range(cols):
        filled = filled | ((row >= t * cap) & (row < t * cap + jnp.minimum(count_ref[0, t], cap)))
    departure = jnp.where(
        filled & (msk_ref[...] > 0),
        wgt_ref[...].astype(jnp.float32) * (radiance - val_ref[...].astype(jnp.float32)),
        0.0,
    )
    dep_ref[...] = departure
    spread_out = dot(departure.astype(jnp.bfloat16), jac_rows, 1)
    increment = jnp.zeros((slots, LANES), jnp.float32)
    for q in range(tiles):
        part = spread_out[:, q * LANES : (q + 1) * LANES]
        increment = increment + jnp.where(row == q * per + lane_group, part, 0.0)
    increment = spread_groups(increment, lev)
    a_all[my_rows, :] = increment * values
    for copy in send(3, "col", cols, me, lambda to: a_all.at[my_rows], a_all.at[my_rows]):
        copy.wait()

    amount = a_all[...]
    a_high, a_low = split(amount)
    a_high, a_low = a_high.astype(jnp.float32), a_low.astype(jnp.float32)
    left = jnp.concatenate([a_high, a_high, a_low, jnp.zeros_like(a_low)], axis=0).T
    left = left[:, 0 : 3 * every].astype(jnp.bfloat16)
    for x in range(cx):
        add = dot(left, wst[x], 0)
        for i, ref in enumerate((ctl, cen.at[0], cen.at[1])):
            for h in halves:
                here = ref.at[h]
                here[picks[x], :] = here[picks[x], :] + add[i * lev : (i + 1) * lev, lanes_of[h]]
    pairs = [(ctl.at[h], octl_hbm.at[:, lanes_of[h]]) for h in halves]
    pairs += [(cen.at[e, h], ocen_hbm.at[e, :, lanes_of[h]]) for e in range(2) for h in halves]
    stores = [pltpu.make_async_copy(src, dst, out_sem.at[i]) for i, (src, dst) in enumerate(pairs)]
    for store in stores:
        store.start()
    for store in stores:
        store.wait()


def fits(members, levels, cells_x, cells_y, slot_total, channels, peers):
    def power(n):
        return n & (n - 1) == 0
    return (
        members == 2 and levels * 4 == LANES and channels == LANES and cells_x == 8
        and cells_y % LANES == 0 and power(cells_y) and cells_y <= 256 and power(peers) and slot_total % 16 == 0
        and power(slot_total // peers) and peers * slot_total * 3 <= 256
        and peers * cells_x > 2 * STEPS
    )


def local_fused(control, control_ens, ensemble, spread, jacobian, obs_value, obs_weight, channel_mask, obs_cell, obs_count):
    members = control_ens.shape[0]
    levels, cells_x, cells_y = control.shape
    slots, _, channels = jacobian.shape
    cols, levs = lax.axis_size("col"), lax.axis_size("lev")
    every = cols * slots
    flat = (levels * cells_x, cells_y)
    cut = (cells_y // LANES, levels * cells_x, LANES)
    any_space = pl.BlockSpec(memory_space=pl.ANY)
    vmem = pl.BlockSpec(memory_space=pltpu.VMEM)
    smem = pl.BlockSpec(memory_space=pltpu.SMEM)
    out_control, out_ens, departures = pl.pallas_call(
        functools.partial(fused, (cols, levs, slots, levels, cells_x, cells_y)),
        out_shape=(
            jax.ShapeDtypeStruct(flat, jnp.float32),
            jax.ShapeDtypeStruct((members,) + flat, jnp.float32),
            jax.ShapeDtypeStruct((slots, channels), jnp.float32),
        ),
        in_specs=[any_space] * 5 + [vmem] * 3 + [smem] * 2,
        out_specs=(any_space, any_space, vmem),
        scratch_shapes=[
            pltpu.VMEM(cut, jnp.float32),
            pltpu.VMEM((members,) + cut, jnp.float32),
            pltpu.VMEM(ensemble.shape, jnp.bfloat16),
            pltpu.VMEM((members,) + cut, jnp.float32),
            pltpu.VMEM(cut, jnp.float32),
            pltpu.VMEM(jacobian.shape, jnp.bfloat16),
            pltpu.VMEM((every, LANES), jnp.int32),
            pltpu.VMEM((STEPS + 1, every, cells_y), jnp.float32),
            pltpu.VMEM((cells_x, 2 * LANES, cells_y), jnp.bfloat16),
            pltpu.VMEM((cells_x, LANES, cells_y), jnp.bfloat16),
            pltpu.VMEM((cells_x, 3 * every, cells_y), jnp.bfloat16),
            pltpu.VMEM((every, 2 * LANES), jnp.float32),
            pltpu.VMEM((cols, slots, 2 * LANES), jnp.float32),
            pltpu.VMEM((levs, slots, LANES), jnp.float32),
            pltpu.VMEM((every, LANES), jnp.float32),
            pltpu.SemaphoreType.DMA((2 + (members + 2) * cut[0],)),
            pltpu.SemaphoreType.DMA(((members + 1) * cut[0],)),
            pltpu.SemaphoreType.DMA((4, max(cols, levs))),
            pltpu.SemaphoreType.DMA((4, max(cols, levs))),
        ],
        compiler_params=pltpu.CompilerParams(
            collective_id=0, has_side_effects=True, vmem_limit_bytes=32 * 1024 * 1024
        ),
    )(
        control.reshape(flat), control_ens.reshape((members,) + flat), ensemble, spread.reshape(flat),
        jacobian, obs_value, obs_weight, channel_mask, obs_cell, obs_count,
    )
    return out_control.reshape(control.shape), out_ens.reshape(control_ens.shape), departures


def pick_local(control, control_ens, ensemble, spread, jacobian, *obs):
    sizes = (control_ens.shape[0],) + control.shape + (jacobian.shape[0], jacobian.shape[2], lax.axis_size("col"))
    run = local_fused if fits(*sizes) else local
    return run(control, control_ens, ensemble, spread, jacobian, *obs)


def solution(mesh):
    placed = (
        P(("grp", "lev"), "col", None),
        P("grp", "lev", "col", None),
        P("grp", "lev", "col", None),
        P(("grp", "lev"), "col", None),
        P(("grp", "col"), "lev", None),
        P(("grp", "col"), None),
        P(("grp", "col"), None),
        P(("grp", "col"), None),
        P(("grp", "col")),
        P(("grp", "col"), None),
    )
    return jax.shard_map(
        pick_local,
        mesh=mesh,
        in_specs=placed,
        out_specs=(
            P(("grp", "lev"), "col", None),
            P("grp", "lev", "col", None),
            P(("grp", "col"), None),
        ),
        check_vma=False,
    )
```

```python
import math

import jax
import jax.numpy as jnp
from jax import lax
from jax.experimental import pallas as pl
from jax.experimental.pallas import tpu as pltpu
from jax.sharding import PartitionSpec as P
import functools
import numpy as np

STEPS = 4


rate_x = 0.35
rate_y = 0.1


def padded_2(value, sides, width):
    for axis, dim in sides:
        peers, length = (lax.axis_size(axis), value.shape[dim])
        up = [(i, (i + 1) % peers) for i in range(peers)]
        down = [(j, i) for i, j in up]
        last = lax.slice_in_dim(value, length - width, length, axis=dim)
        initial = lax.slice_in_dim(value, 0, width, axis=dim)
        before = lax.ppermute(last, axis, up)
        after = lax.ppermute(initial, axis, down)
        value = jnp.concatenate([before, value, after], axis=dim)
    return value


def smooth(fields):
    for iteration in range(STEPS):
        padded = padded_2(fields, (("col", 2),), 1)
        beside = jnp.pad(fields, ((0, 0), (0, 0), (0, 0), (1, 1)))
        along_x = padded[:, :, 2:, :] + padded[:, :, :-2, :] - 2.0 * fields
        along_y = beside[..., 2:] + beside[..., :-2] - 2.0 * fields
        fields = fields + rate_x * along_x + rate_y * along_y
    return fields


def solve_rows(jac_rows, columns, values, weights, masks, filled):
    partial_value = jnp.einsum("rlc,rl->rc", jac_rows, columns, preferred_element_type=jnp.float32)
    radiance = lax.psum(partial_value, "lev")
    active = (filled[:, None] > 0) & (masks > 0)
    departure = jnp.where(
        active, weights.astype(jnp.float32) * (radiance - values.astype(jnp.float32)), 0.0
    )
    increment = jnp.einsum(
        "rc,rlc->rl", departure.astype(jnp.bfloat16), jac_rows, preferred_element_type=jnp.float32
    )
    return (departure, increment)


def local(
    control,
    control_ens,
    ensemble,
    spread,
    jacobian,
    obs_value,
    obs_weight,
    channel_mask,
    obs_cell,
    obs_count,
):
    members = control_ens.shape[0]
    ens_scale = 1.0 / math.sqrt(members)
    levels, cells_x, cells_y = control.shape
    peer_count = lax.axis_size("col")
    slot_total = jacobian.shape[0]
    capacity = slot_total // peer_count
    smoothed = smooth(jnp.concatenate([control[None], control_ens], 0))
    analysis = spread * smoothed[0] + jnp.sum(ensemble * smoothed[1:], 0) * ens_scale
    flat_state = analysis.reshape(levels, cells_x * cells_y)
    row_ids = jnp.arange(slot_total, dtype=jnp.int32)
    target = row_ids // capacity
    slot_index = row_ids % capacity
    filled = (slot_index < obs_count[0][target]).astype(jnp.int32)
    empty_grid = jnp.zeros((levels, cells_x * cells_y), jnp.float32)
    jac_recv, value_recv, weight_recv, mask_recv, cell_recv, filled_recv = (
        lax.all_to_all(jacobian, "col", split_axis=0, concat_axis=0, tiled=True),
        lax.all_to_all(obs_value, "col", split_axis=0, concat_axis=0, tiled=True),
        lax.all_to_all(obs_weight, "col", split_axis=0, concat_axis=0, tiled=True),
        lax.all_to_all(channel_mask, "col", split_axis=0, concat_axis=0, tiled=True),
        lax.all_to_all(obs_cell, "col", split_axis=0, concat_axis=0, tiled=True),
        lax.all_to_all(filled, "col", split_axis=0, concat_axis=0, tiled=True),
    )
    columns = flat_state[:, cell_recv].T.astype(jnp.bfloat16)
    departure, increment = solve_rows(
        jac_recv, columns, value_recv, weight_recv, mask_recv, filled_recv
    )
    gradient_flat = empty_grid.at[:, cell_recv].add(increment.T)
    departures = lax.all_to_all(departure, "col", split_axis=0, concat_axis=0, tiled=True)
    gradient_field = gradient_flat.reshape(levels, cells_x, cells_y)
    adjoint = smooth(
        jnp.concatenate(
            [(spread * gradient_field)[None], ensemble * gradient_field[None] * ens_scale], 0
        )
    )
    return (control + adjoint[0], control_ens + adjoint[1:], departures)


LANES = 128


def stencil_power():
    step = np.array([[0.0, rate_x, 0.0], [rate_y, 1.0 - 2.0 * rate_x - 2.0 * rate_y, rate_y], [0.0, rate_x, 0.0]])
    total = np.zeros((2 * STEPS + 1, 2 * STEPS + 1))
    total[STEPS, STEPS] = 1.0
    for _ in range(STEPS):
        wide = np.pad(total, 1)
        total = sum(
            step[i, j] * wide[i : i + 2 * STEPS + 1, j : j + 2 * STEPS + 1]
            for i in range(3)
            for j in range(3)
        )
    return total[STEPS:, STEPS:]


def split(value):
    high = value.astype(jnp.bfloat16)
    return high, (value - high.astype(jnp.float32)).astype(jnp.bfloat16)


def dot(a, b, b_dim):
    return lax.dot_general(a, b, (((1,), (b_dim,)), ((), ())), preferred_element_type=jnp.float32)


def spread_groups(value, width):
    total = value
    for shift in range(width, LANES, width):
        total = total + pltpu.roll(value, shift, 1)
    return total


def fused(
    cfg,
    ctl_hbm, cen_hbm, ens_hbm, spr_hbm, jac_hbm, val_hbm, wgt_hbm, msk_hbm, cell_hbm, count_hbm,
    wst_hbm, a_hbm, dep_hbm,
    ctl, cen, ens, ensf, spr, jac, val_ref, wgt_ref, msk_ref, cell_ref, count_ref, cells, dep_ref, ey, fst, vst, wst, found_ref, pv, pv_in, rad_in, a_all,
    in_sem, out_sem, send_sem, recv_sem,
):
    cols, levs, slots, lev, cx, ny = cfg
    cap = slots // cols
    nx = cols * cx
    every = cols * slots
    me, my_lev = lax.axis_index("col"), lax.axis_index("lev")
    table = stencil_power()
    parts = slots // max(8, cap)

    halves = range(ny // LANES)
    lanes_of = [slice(h * LANES, (h + 1) * LANES) for h in halves]
    pairs = [(ctl_hbm.at[:, lanes_of[h]], ctl.at[h]) for h in halves]
    pairs += [(cen_hbm.at[e, :, lanes_of[h]], cen.at[e, h]) for e in range(2) for h in halves]
    fields = len(pairs)
    pairs += [(ens_hbm, ens)] + [(spr_hbm.at[:, lanes_of[h]], spr.at[h]) for h in halves]
    small = len(pairs)
    pairs += [(jac_hbm, jac), (val_hbm, val_ref), (wgt_hbm, wgt_ref), (msk_hbm, msk_ref), (count_hbm, count_ref)]
    pairs += [(cell_hbm, cell_ref)]
    loads = [pltpu.make_async_copy(src, dst, in_sem.at[i]) for i, (src, dst) in enumerate(pairs)]
    loads[-1].start()
    barrier = pltpu.get_barrier_semaphore()
    for d in range(1, cols):
        pl.semaphore_signal(
            barrier, inc=1, device_id={"col": lax.rem(me + d, cols)}, device_id_type=pl.DeviceIdType.MESH
        )
    for d in range(1, levs):
        pl.semaphore_signal(
            barrier, inc=1, device_id={"lev": lax.rem(my_lev + d, levs)}, device_id_type=pl.DeviceIdType.MESH
        )

    for load in loads[:-1]:
        load.start()

    def send(phase, axis, peers, mine, src_of, dst):
        copies = []
        for d in range(1, peers):
            to = lax.rem(mine + d, peers)
            copy = pltpu.make_async_remote_copy(
                src_ref=src_of(to),
                dst_ref=dst,
                send_sem=send_sem.at[phase, d],
                recv_sem=recv_sem.at[phase, d],
                device_id={axis: to},
                device_id_type=pl.DeviceIdType.MESH,
            )
            copy.start()
            copies.append(copy)
        return copies

    loads[-1].wait()
    row = lax.broadcasted_iota(jnp.int32, (slots, LANES), 0)
    lane = lax.broadcasted_iota(jnp.int32, (slots, LANES), 1)
    own = jnp.zeros((slots, LANES), jnp.int32)
    for r in range(slots):
        own = jnp.where(row == r, cell_ref[r], own)
    my_rows = pl.ds(pl.multiple_of(me * slots, slots), slots)
    cells[my_rows, :] = own
    pl.semaphore_wait(barrier, cols + levs - 2)
    cell_copies = send(0, "col", cols, me, lambda to: cells.at[my_rows], cells.at[my_rows])

    for load in loads[:fields]:
        load.wait()
    zeros = jnp.zeros((lev, ny), jnp.bfloat16)
    picks = [pl.ds(x, lev, stride=cx) for x in range(cx)]
    for x in range(cx):
        for i, ref in enumerate((ctl, cen.at[0], cen.at[1])):
            for h in halves:
                high, low = split(ref.at[h][picks[x], :])
                fst[x, i * lev : (i + 1) * lev, lanes_of[h]] = high
                fst[x, LANES + i * lev : LANES + (i + 1) * lev, lanes_of[h]] = low
        fst[x, 3 * lev : 4 * lev, :] = zeros
        fst[x, LANES + 3 * lev : LANES + 4 * lev, :] = zeros
    for load in loads[fields:small]:
        load.wait()
    for e in range(2):
        member = ens[e].astype(jnp.float32).reshape(lev * cx, ny)
        for h in halves:
            ensf[e, h] = member[:, lanes_of[h]]
    for x in range(cx):
        for h in halves:
            high, low = split(spr.at[h][picks[x], :])
            vst[x, 0:lev, lanes_of[h]] = high
            vst[x, lev : 2 * lev, lanes_of[h]] = ensf.at[0, h][picks[x], :].astype(jnp.bfloat16)
            vst[x, 2 * lev : 3 * lev, lanes_of[h]] = ensf.at[1, h][picks[x], :].astype(jnp.bfloat16)
            vst[x, 3 * lev : 4 * lev, lanes_of[h]] = low

    for copy in cell_copies:
        copy.wait()

    cell = cells[...]
    shift = ny.bit_length() - 1
    cell_x = lax.shift_right_logical(cell, jnp.full_like(cell, shift))
    cell_y = cell & (ny - 1)
    slot = lax.broadcasted_iota(jnp.int32, (every, LANES), 0)
    target = lax.shift_right_logical(slot, jnp.full_like(slot, cap.bit_length() - 1)) & (cols - 1)
    apart = me * cx - (target * cx + cell_x)
    y_lane = lax.broadcasted_iota(jnp.int32, (every, LANES), 1)
    for h in range(ny // LANES):
        y = y_lane + h * LANES
        dy = jnp.abs(y - cell_y)
        below = y + cell_y + 2
        above = 2 * ny - y - cell_y
        for m in range(STEPS + 1):
            one = jnp.where(dy == m, 1.0, 0.0)
            if m >= 2:
                one = one - jnp.where((below == m) | (above == m), 1.0, 0.0)
            ey[m, :, h * LANES : (h + 1) * LANES] = one
    out = None
    for x in range(cx):
        dx = apart + x
        dx = jnp.where(dx >= nx // 2, dx - nx, dx)
        dx = jnp.abs(jnp.where(dx < -(nx // 2), dx + nx, dx))
        at = [dx == q for q in range(STEPS + 1)]
        factors = []
        for m in range(STEPS + 1):
            factor = jnp.zeros((every, LANES), jnp.float32)
            for q in range(STEPS + 1 - m):
                factor = jnp.where(at[q], float(table[q, m]), factor)
            factors.append(factor)
        here = jnp.where(at[0], 1.0, 0.0)
        hits = []
        for h in range(ny // LANES):
            part = slice(h * LANES, (h + 1) * LANES)
            centre = ey[0, :, part]
            weight = factors[0] * centre
            for m in range(1, STEPS + 1):
                weight = weight + factors[m] * ey[m, :, part]
            high, low = split(weight)
            wst[x, 0:every, part] = high
            wst[x, every : 2 * every, part] = low
            wst[x, 2 * every : 3 * every, part] = high
            hits.append((here * centre).astype(jnp.bfloat16))
        sums = dot(wst[x, 0 : 2 * every, :], fst[x], 1)
        found = dot(jnp.concatenate(hits, axis=1), vst[x], 1)
        out = (sums, found) if out is None else (out[0] + sums, out[1] + found)
    sums, found = out
    wst_store = pltpu.make_async_copy(wst, wst_hbm, out_sem.at[0])
    wst_store.start()
    sums = sums[0:every, 0:LANES] + sums[0:every, LANES:] + sums[every:, 0:LANES]
    group = lax.shift_right_logical(y_lane, jnp.full_like(y_lane, lev.bit_length() - 1))
    found = jnp.where(group == 0, found + pltpu.roll(found, lev, 1), found * (1.0 / math.sqrt(2)))
    found_ref[...] = jnp.where(group == 3, 0.0, found)
    window = slots // parts
    for s in range(cols):
        pv[s, 0:slots, :] = sums[s * slots : (s + 1) * slots]
        start = s * slots + lax.div(me * cap, window) * window
        pv[s, slots:, :] = found_ref[pl.ds(pl.multiple_of(start, window), window), :]
    pv_in[me] = pv[me]
    copies = send(1, "col", cols, me, lambda to: pv.at[to], pv_in.at[me])
    for load in loads[small:-1]:
        load.wait()
    for copy in copies:
        copy.wait()

    fields_at = pv_in[0, 0:slots, :]
    for s in range(1, cols):
        fields_at = fields_at + pv_in[s, 0:slots, :]
    per_part = cols // parts
    pieces = []
    for p in range(parts):
        piece = pv_in[p * per_part, slots:, :]
        for s in range(p * per_part + 1, (p + 1) * per_part):
            piece = piece + pv_in[s, slots:, :]
        pieces.append(piece)
    values = jnp.concatenate(pieces, axis=0) if parts > 1 else pieces[0]
    columns = spread_groups(fields_at * values, lev)
    jac_rows = jac[...].reshape(slots * lev, LANES)
    per = LANES // lev
    lane_group = lax.shift_right_logical(lane, jnp.full_like(lane, lev.bit_length() - 1))
    tiles = slots // per
    block = jnp.concatenate(
        [jnp.where(row == q * per + lane_group, columns, 0.0) for q in range(tiles)], axis=1
    ).astype(jnp.bfloat16)
    rad_in[my_lev] = dot(block, jac_rows, 0)
    for copy in send(2, "lev", levs, my_lev, lambda to: rad_in.at[my_lev], rad_in.at[my_lev]):
        copy.wait()
    radiance = rad_in[0]
    for s in range(1, levs):
        radiance = radiance + rad_in[s]

    filled = jnp.zeros((slots, LANES), jnp.bool_)
    for t in range(cols):
        filled = filled | ((row >= t * cap) & (row < t * cap + jnp.minimum(count_ref[0, t], cap)))
    departure = jnp.where(
        filled & (msk_ref[...] > 0),
        wgt_ref[...].astype(jnp.float32) * (radiance - val_ref[...].astype(jnp.float32)),
        0.0,
    )
    dep_ref[...] = departure
    dep_store = pltpu.make_async_copy(dep_ref, dep_hbm, out_sem.at[out_sem.shape[0] - 1])
    dep_store.start()
    spread_out = dot(departure.astype(jnp.bfloat16), jac_rows, 1)
    increment = jnp.zeros((slots, LANES), jnp.float32)
    for q in range(tiles):
        part = spread_out[:, q * LANES : (q + 1) * LANES]
        increment = increment + jnp.where(row == q * per + lane_group, part, 0.0)
    increment = spread_groups(increment, lev)
    a_all[my_rows, :] = increment * values
    for copy in send(3, "col", cols, me, lambda to: a_all.at[my_rows], a_all.at[my_rows]):
        copy.wait()

    a_store = pltpu.make_async_copy(a_all, a_hbm, out_sem.at[1])
    a_store.start()
    for store in (wst_store, a_store, dep_store):
        store.wait()


def adjoint(
    cfg, ctl_hbm, cen_hbm, wst_hbm, a_hbm, dep_hbm, octl_hbm, ocen_hbm, odep_hbm,
    ctl, cen, wst, amount, dep, in_sem, out_sem,
):
    lev, cx, ny = cfg
    halves = range(ny // LANES)
    lanes_of = [slice(h * LANES, (h + 1) * LANES) for h in halves]
    pairs = [(a_hbm, amount), (wst_hbm, wst)]
    for h in halves:
        pairs += [(ctl_hbm.at[:, lanes_of[h]], ctl.at[h])]
        pairs += [(cen_hbm.at[e, :, lanes_of[h]], cen.at[e, h]) for e in range(2)]
    pairs += [(dep_hbm, dep)]
    loads = [pltpu.make_async_copy(src, dst, in_sem.at[i]) for i, (src, dst) in enumerate(pairs)]
    for load in loads:
        load.start()
    loads[0].wait()
    every = amount.shape[0]
    a_high, a_low = split(amount[...])
    a_high, a_low = a_high.astype(jnp.float32), a_low.astype(jnp.float32)
    left = jnp.concatenate([a_high, a_high, a_low, jnp.zeros_like(a_low)], axis=0).T
    left = left[:, 0 : 3 * every].astype(jnp.bfloat16)
    loads[1].wait()
    stores = []
    for h in halves:
        for load in loads[2 + 3 * h : 5 + 3 * h]:
            load.wait()
        for x in range(cx):
            pick = pl.ds(x, lev, stride=cx)
            add = dot(left, wst[x, :, lanes_of[h]], 0)
            for i, ref in enumerate((ctl.at[h], cen.at[0, h], cen.at[1, h])):
                ref[pick, :] = ref[pick, :] + add[i * lev : (i + 1) * lev]
        pairs = [(ctl.at[h], octl_hbm.at[:, lanes_of[h]])]
        pairs += [(cen.at[e, h], ocen_hbm.at[e, :, lanes_of[h]]) for e in range(2)]
        for src, dst in pairs:
            stores.append(pltpu.make_async_copy(src, dst, out_sem.at[len(stores)]))
            stores[-1].start()
    loads[-1].wait()
    stores.append(pltpu.make_async_copy(dep, odep_hbm, out_sem.at[len(stores)]))
    stores[-1].start()
    for store in stores:
        store.wait()


def fits(members, levels, cells_x, cells_y, slot_total, channels, peers):
    def power(n):
        return n & (n - 1) == 0
    return (
        members == 2 and levels * 4 == LANES and channels == LANES and cells_x == 8
        and cells_y % LANES == 0 and power(cells_y) and cells_y <= 256 and power(peers) and slot_total % 16 == 0
        and power(slot_total // peers) and peers * slot_total * 3 <= 256
        and peers * cells_x > 2 * STEPS
    )


def local_fused(control, control_ens, ensemble, spread, jacobian, obs_value, obs_weight, channel_mask, obs_cell, obs_count):
    members = control_ens.shape[0]
    levels, cells_x, cells_y = control.shape
    slots, _, channels = jacobian.shape
    cols, levs = lax.axis_size("col"), lax.axis_size("lev")
    every = cols * slots
    flat = (levels * cells_x, cells_y)
    cut = (cells_y // LANES, levels * cells_x, LANES)
    hbm = pl.BlockSpec(memory_space=pltpu.HBM)
    weights, amount, held = pl.pallas_call(
        functools.partial(fused, (cols, levs, slots, levels, cells_x, cells_y)),
        out_shape=(
            jax.ShapeDtypeStruct((cells_x, 3 * every, cells_y), jnp.bfloat16),
            jax.ShapeDtypeStruct((every, LANES), jnp.float32),
            jax.ShapeDtypeStruct((slots, channels), jnp.float32),
        ),
        in_specs=[hbm] * 10,
        out_specs=(hbm, hbm, hbm),
        scratch_shapes=[
            pltpu.VMEM(cut, jnp.float32),
            pltpu.VMEM((members,) + cut, jnp.float32),
            pltpu.VMEM(ensemble.shape, jnp.bfloat16),
            pltpu.VMEM((members,) + cut, jnp.float32),
            pltpu.VMEM(cut, jnp.float32),
            pltpu.VMEM(jacobian.shape, jnp.bfloat16),
            pltpu.VMEM(obs_value.shape, jnp.bfloat16),
            pltpu.VMEM(obs_weight.shape, jnp.bfloat16),
            pltpu.VMEM(channel_mask.shape, jnp.int32),
            pltpu.SMEM(obs_cell.shape, jnp.int32),
            pltpu.SMEM(obs_count.shape, jnp.int32),
            pltpu.VMEM((every, LANES), jnp.int32),
            pltpu.VMEM((slots, channels), jnp.float32),
            pltpu.VMEM((STEPS + 1, every, cells_y), jnp.float32),
            pltpu.VMEM((cells_x, 2 * LANES, cells_y), jnp.bfloat16),
            pltpu.VMEM((cells_x, LANES, cells_y), jnp.bfloat16),
            pltpu.VMEM((cells_x, 3 * every, cells_y), jnp.bfloat16),
            pltpu.VMEM((every, LANES), jnp.float32),
            pltpu.VMEM((cols, slots + max(8, slots // cols), LANES), jnp.float32),
            pltpu.VMEM((cols, slots + max(8, slots // cols), LANES), jnp.float32),
            pltpu.VMEM((levs, slots, LANES), jnp.float32),
            pltpu.VMEM((every, LANES), jnp.float32),
            pltpu.SemaphoreType.DMA((7 + (members + 2) * cut[0],)),
            pltpu.SemaphoreType.DMA((3,)),
            pltpu.SemaphoreType.DMA((4, max(cols, levs))),
            pltpu.SemaphoreType.DMA((4, max(cols, levs))),
        ],
        compiler_params=pltpu.CompilerParams(
            collective_id=0, has_side_effects=True, vmem_limit_bytes=63 * 1024 * 1024
        ),
    )(
        control.reshape(flat), control_ens.reshape((members,) + flat), ensemble, spread.reshape(flat),
        jacobian, obs_value, obs_weight, channel_mask, obs_cell, obs_count,
    )
    out_control, out_ens, departures = pl.pallas_call(
        functools.partial(adjoint, (levels, cells_x, cells_y)),
        out_shape=(
            jax.ShapeDtypeStruct(flat, jnp.float32),
            jax.ShapeDtypeStruct((members,) + flat, jnp.float32),
            jax.ShapeDtypeStruct((slots, channels), jnp.float32),
        ),
        in_specs=[hbm] * 5,
        out_specs=(hbm,) * 3,
        scratch_shapes=[
            pltpu.VMEM(cut, jnp.float32),
            pltpu.VMEM((members,) + cut, jnp.float32),
            pltpu.VMEM((cells_x, 3 * every, cells_y), jnp.bfloat16),
            pltpu.VMEM((every, LANES), jnp.float32),
            pltpu.VMEM((slots, channels), jnp.float32),
            pltpu.SemaphoreType.DMA((3 + (members + 1) * cut[0],)),
            pltpu.SemaphoreType.DMA((1 + (members + 1) * cut[0],)),
        ],
        compiler_params=pltpu.CompilerParams(vmem_limit_bytes=63 * 1024 * 1024),
    )(control.reshape(flat), control_ens.reshape((members,) + flat), weights, amount, held)
    return out_control.reshape(control.shape), out_ens.reshape(control_ens.shape), departures


def pick_local(control, control_ens, ensemble, spread, jacobian, *obs):
    sizes = (control_ens.shape[0],) + control.shape + (jacobian.shape[0], jacobian.shape[2], lax.axis_size("col"))
    run = local_fused if fits(*sizes) else local
    return run(control, control_ens, ensemble, spread, jacobian, *obs)


def solution(mesh):
    placed = (
        P(("grp", "lev"), "col", None),
        P("grp", "lev", "col", None),
        P("grp", "lev", "col", None),
        P(("grp", "lev"), "col", None),
        P(("grp", "col"), "lev", None),
        P(("grp", "col"), None),
        P(("grp", "col"), None),
        P(("grp", "col"), None),
        P(("grp", "col")),
        P(("grp", "col"), None),
    )
    return jax.shard_map(
        pick_local,
        mesh=mesh,
        in_specs=placed,
        out_specs=(
            P(("grp", "lev"), "col", None),
            P("grp", "lev", "col", None),
            P(("grp", "col"), None),
        ),
        check_vma=False,
    )
```

```python
import math

import jax
import jax.numpy as jnp
from jax import lax
from jax.experimental import pallas as pl
from jax.experimental.pallas import tpu as pltpu
from jax.sharding import PartitionSpec as P
import functools
import numpy as np

STEPS = 4


rate_x = 0.35
rate_y = 0.1


def padded_2(value, sides, width):
    for axis, dim in sides:
        peers, length = (lax.axis_size(axis), value.shape[dim])
        up = [(i, (i + 1) % peers) for i in range(peers)]
        down = [(j, i) for i, j in up]
        last = lax.slice_in_dim(value, length - width, length, axis=dim)
        initial = lax.slice_in_dim(value, 0, width, axis=dim)
        before = lax.ppermute(last, axis, up)
        after = lax.ppermute(initial, axis, down)
        value = jnp.concatenate([before, value, after], axis=dim)
    return value


def smooth(fields):
    for iteration in range(STEPS):
        padded = padded_2(fields, (("col", 2),), 1)
        beside = jnp.pad(fields, ((0, 0), (0, 0), (0, 0), (1, 1)))
        along_x = padded[:, :, 2:, :] + padded[:, :, :-2, :] - 2.0 * fields
        along_y = beside[..., 2:] + beside[..., :-2] - 2.0 * fields
        fields = fields + rate_x * along_x + rate_y * along_y
    return fields


def solve_rows(jac_rows, columns, values, weights, masks, filled):
    partial_value = jnp.einsum("rlc,rl->rc", jac_rows, columns, preferred_element_type=jnp.float32)
    radiance = lax.psum(partial_value, "lev")
    active = (filled[:, None] > 0) & (masks > 0)
    departure = jnp.where(
        active, weights.astype(jnp.float32) * (radiance - values.astype(jnp.float32)), 0.0
    )
    increment = jnp.einsum(
        "rc,rlc->rl", departure.astype(jnp.bfloat16), jac_rows, preferred_element_type=jnp.float32
    )
    return (departure, increment)


def local(
    control,
    control_ens,
    ensemble,
    spread,
    jacobian,
    obs_value,
    obs_weight,
    channel_mask,
    obs_cell,
    obs_count,
):
    members = control_ens.shape[0]
    ens_scale = 1.0 / math.sqrt(members)
    levels, cells_x, cells_y = control.shape
    peer_count = lax.axis_size("col")
    slot_total = jacobian.shape[0]
    capacity = slot_total // peer_count
    smoothed = smooth(jnp.concatenate([control[None], control_ens], 0))
    analysis = spread * smoothed[0] + jnp.sum(ensemble * smoothed[1:], 0) * ens_scale
    flat_state = analysis.reshape(levels, cells_x * cells_y)
    row_ids = jnp.arange(slot_total, dtype=jnp.int32)
    target = row_ids // capacity
    slot_index = row_ids % capacity
    filled = (slot_index < obs_count[0][target]).astype(jnp.int32)
    empty_grid = jnp.zeros((levels, cells_x * cells_y), jnp.float32)
    jac_recv, value_recv, weight_recv, mask_recv, cell_recv, filled_recv = (
        lax.all_to_all(jacobian, "col", split_axis=0, concat_axis=0, tiled=True),
        lax.all_to_all(obs_value, "col", split_axis=0, concat_axis=0, tiled=True),
        lax.all_to_all(obs_weight, "col", split_axis=0, concat_axis=0, tiled=True),
        lax.all_to_all(channel_mask, "col", split_axis=0, concat_axis=0, tiled=True),
        lax.all_to_all(obs_cell, "col", split_axis=0, concat_axis=0, tiled=True),
        lax.all_to_all(filled, "col", split_axis=0, concat_axis=0, tiled=True),
    )
    columns = flat_state[:, cell_recv].T.astype(jnp.bfloat16)
    departure, increment = solve_rows(
        jac_recv, columns, value_recv, weight_recv, mask_recv, filled_recv
    )
    gradient_flat = empty_grid.at[:, cell_recv].add(increment.T)
    departures = lax.all_to_all(departure, "col", split_axis=0, concat_axis=0, tiled=True)
    gradient_field = gradient_flat.reshape(levels, cells_x, cells_y)
    adjoint = smooth(
        jnp.concatenate(
            [(spread * gradient_field)[None], ensemble * gradient_field[None] * ens_scale], 0
        )
    )
    return (control + adjoint[0], control_ens + adjoint[1:], departures)


LANES = 128


def stencil_power():
    step = np.array([[0.0, rate_x, 0.0], [rate_y, 1.0 - 2.0 * rate_x - 2.0 * rate_y, rate_y], [0.0, rate_x, 0.0]])
    total = np.zeros((2 * STEPS + 1, 2 * STEPS + 1))
    total[STEPS, STEPS] = 1.0
    for _ in range(STEPS):
        wide = np.pad(total, 1)
        total = sum(
            step[i, j] * wide[i : i + 2 * STEPS + 1, j : j + 2 * STEPS + 1]
            for i in range(3)
            for j in range(3)
        )
    return total[STEPS:, STEPS:]


def split(value):
    high = value.astype(jnp.bfloat16)
    return high, (value - high.astype(jnp.float32)).astype(jnp.bfloat16)


def dot(a, b, b_dim):
    return lax.dot_general(a, b, (((1,), (b_dim,)), ((), ())), preferred_element_type=jnp.float32)


def spread_groups(value, width):
    total = value
    for shift in range(width, LANES, width):
        total = total + pltpu.roll(value, shift, 1)
    return total


def fused(
    cfg,
    ctl_hbm, cen_hbm, ens_hbm, spr_hbm, jac_hbm, val_hbm, wgt_hbm, msk_hbm, cell_hbm, count_hbm,
    wst_hbm, a_hbm, dep_hbm,
    ctl, cen, ens, ensf, spr, jac, val_ref, wgt_ref, msk_ref, cell_ref, count_ref, cells, dep_ref, ey, fst, vst, wst, pv, pv_in, dep_in, a_out, a_in, a_all,
    in_sem, out_sem, send_sem, recv_sem,
):
    cols, levs, slots, lev, cx, ny = cfg
    cap = slots // cols
    nx = cols * cx
    every = cols * slots
    me, my_lev = lax.axis_index("col"), lax.axis_index("lev")
    table = stencil_power()

    halves = range(ny // LANES)
    lanes_of = [slice(h * LANES, (h + 1) * LANES) for h in halves]
    pairs = [(ctl_hbm.at[:, lanes_of[h]], ctl.at[h]) for h in halves]
    pairs += [(cen_hbm.at[e, :, lanes_of[h]], cen.at[e, h]) for e in range(2) for h in halves]
    fields = len(pairs)
    pairs += [(ens_hbm, ens)] + [(spr_hbm.at[:, lanes_of[h]], spr.at[h]) for h in halves]
    small = len(pairs)
    pairs += [(jac_hbm.at[pl.ds(my_lev * (slots // levs), slots // levs)], jac.at[my_lev]), (val_hbm, val_ref), (wgt_hbm, wgt_ref), (msk_hbm, msk_ref), (count_hbm, count_ref)]
    pairs += [(cell_hbm, cell_ref)]
    loads = [pltpu.make_async_copy(src, dst, in_sem.at[i]) for i, (src, dst) in enumerate(pairs)]
    loads[-1].start()
    barrier = pltpu.get_barrier_semaphore()
    peers = cols * levs
    my_id = me * levs + my_lev
    for d in range(1, peers):
        to = lax.rem(my_id + d, peers)
        pl.semaphore_signal(
            barrier, inc=1, device_id={"col": lax.div(to, levs), "lev": lax.rem(to, levs)},
            device_id_type=pl.DeviceIdType.MESH,
        )
    for load in loads[:-1]:
        load.start()

    def send(phase, axis, src_of, dst):
        count, mine = {"col": (cols, me), "lev": (levs, my_lev), "all": (peers, my_id)}[axis]
        copies = []
        for d in range(1, count):
            to = lax.rem(mine + d, count)
            device = {"col": lax.div(to, levs), "lev": lax.rem(to, levs)} if axis == "all" else {axis: to}
            copy = pltpu.make_async_remote_copy(
                src_ref=src_of(to),
                dst_ref=dst,
                send_sem=send_sem.at[phase, d],
                recv_sem=recv_sem.at[phase, d],
                device_id=device,
                device_id_type=pl.DeviceIdType.MESH,
            )
            copy.start()
            copies.append(copy)
        return copies

    loads[-1].wait()
    row = lax.broadcasted_iota(jnp.int32, (slots, LANES), 0)
    lane = lax.broadcasted_iota(jnp.int32, (slots, LANES), 1)
    own = jnp.zeros((slots, LANES), jnp.int32)
    for r in range(slots):
        own = jnp.where(row == r, cell_ref[r], own)
    my_rows = pl.ds(pl.multiple_of(me * slots, slots), slots)
    cells[my_rows, :] = own
    pl.semaphore_wait(barrier, peers - 1)
    cell_copies = send(0, "col", lambda to: cells.at[my_rows], cells.at[my_rows])
    share = slots // levs
    jac_copies = send(2, "lev", lambda to: jac_hbm.at[pl.ds(to * share, share)], jac.at[my_lev])

    for load in loads[:fields]:
        load.wait()
    zeros = jnp.zeros((lev, ny), jnp.bfloat16)
    picks = [pl.ds(x, lev, stride=cx) for x in range(cx)]
    for x in range(cx):
        for i, ref in enumerate((ctl, cen.at[0], cen.at[1])):
            for h in halves:
                high, low = split(ref.at[h][picks[x], :])
                fst[x, i * lev : (i + 1) * lev, lanes_of[h]] = high
                fst[x, LANES + i * lev : LANES + (i + 1) * lev, lanes_of[h]] = low
        fst[x, 3 * lev : 4 * lev, :] = zeros
        fst[x, LANES + 3 * lev : LANES + 4 * lev, :] = zeros
    for load in loads[fields:small]:
        load.wait()
    for e in range(2):
        member = ens[e].astype(jnp.float32).reshape(lev * cx, ny)
        for h in halves:
            ensf[e, h] = member[:, lanes_of[h]]
    for x in range(cx):
        for h in halves:
            high, low = split(spr.at[h][picks[x], :])
            vst[x, 0:lev, lanes_of[h]] = high
            vst[x, lev : 2 * lev, lanes_of[h]] = ensf.at[0, h][picks[x], :].astype(jnp.bfloat16)
            vst[x, 2 * lev : 3 * lev, lanes_of[h]] = ensf.at[1, h][picks[x], :].astype(jnp.bfloat16)
            vst[x, 3 * lev : 4 * lev, lanes_of[h]] = low

    for copy in cell_copies:
        copy.wait()

    cell = cells[...]
    shift = ny.bit_length() - 1
    cell_x = lax.shift_right_logical(cell, jnp.full_like(cell, shift))
    cell_y = cell & (ny - 1)
    slot = lax.broadcasted_iota(jnp.int32, (every, LANES), 0)
    target = lax.shift_right_logical(slot, jnp.full_like(slot, cap.bit_length() - 1)) & (cols - 1)
    apart = me * cx - (target * cx + cell_x)
    y_lane = lax.broadcasted_iota(jnp.int32, (every, LANES), 1)
    for h in range(ny // LANES):
        y = y_lane + h * LANES
        dy = jnp.abs(y - cell_y)
        below = y + cell_y + 2
        above = 2 * ny - y - cell_y
        for m in range(STEPS + 1):
            one = jnp.where(dy == m, 1.0, 0.0)
            if m >= 2:
                one = one - jnp.where((below == m) | (above == m), 1.0, 0.0)
            ey[m, :, h * LANES : (h + 1) * LANES] = one
    out = None
    for x in range(cx):
        dx = apart + x
        dx = jnp.where(dx >= nx // 2, dx - nx, dx)
        dx = jnp.abs(jnp.where(dx < -(nx // 2), dx + nx, dx))
        at = [dx == q for q in range(STEPS + 1)]
        factors = []
        for m in range(STEPS + 1):
            factor = jnp.zeros((every, LANES), jnp.float32)
            for q in range(STEPS + 1 - m):
                factor = jnp.where(at[q], float(table[q, m]), factor)
            factors.append(factor)
        here = jnp.where(at[0], 1.0, 0.0)
        hits = []
        for h in range(ny // LANES):
            part = slice(h * LANES, (h + 1) * LANES)
            centre = ey[0, :, part]
            weight = factors[0] * centre
            for m in range(1, STEPS + 1):
                weight = weight + factors[m] * ey[m, :, part]
            high, low = split(weight)
            wst[x, 0:every, part] = high
            wst[x, every : 2 * every, part] = low
            wst[x, 2 * every : 3 * every, part] = high
            hits.append((here * centre).astype(jnp.bfloat16))
        sums = dot(wst[x, 0 : 2 * every, :], fst[x], 1)
        found = dot(jnp.concatenate(hits, axis=1), vst[x], 1)
        out = (sums, found) if out is None else (out[0] + sums, out[1] + found)
    sums, found = out
    wst_store = pltpu.make_async_copy(wst, wst_hbm, out_sem.at[0])
    wst_store.start()
    sums = sums[0:every, 0:LANES] + sums[0:every, LANES:] + sums[every:, 0:LANES]
    group = lax.shift_right_logical(y_lane, jnp.full_like(y_lane, lev.bit_length() - 1))
    found = jnp.where(group == 0, found + pltpu.roll(found, lev, 1), found * (1.0 / math.sqrt(2)))
    found = jnp.where(group == 3, 0.0, found)
    for q in range(peers):
        pv[q, 0:share, :] = sums[q * share : (q + 1) * share]
        pv[q, share:, :] = found[q * share : (q + 1) * share]
    pv_in[my_id] = pv[my_id]
    copies = send(1, "all", lambda to: pv.at[to], pv_in.at[my_id])
    for load in loads[small:-1]:
        load.wait()
    for copy in jac_copies + copies:
        copy.wait()

    row = lax.broadcasted_iota(jnp.int32, (2 * share, LANES), 0)
    lane = lax.broadcasted_iota(jnp.int32, (2 * share, LANES), 1)
    own_lane = lax.shift_right_logical(lane, jnp.full_like(lane, lev.bit_length() - 1)) == (row & (share - 1))
    values, blocks = [], []
    for j in range(levs):
        both = pv_in[j]
        for s in range(1, cols):
            both = both + pv_in[s * levs + j]
        turned = pltpu.roll(both, share, 0)
        values.append(jnp.where(row < share, turned, both))
        blocks.append(jnp.where(own_lane, spread_groups(both * turned, lev), 0.0))
    jac_rows = jac[...].reshape(slots * lev, LANES)
    block = jnp.concatenate([jnp.concatenate(blocks, axis=1)] * 2, axis=0).astype(jnp.bfloat16)
    radiance = dot(block, jac_rows, 0)[0 : 2 * share]

    slot_in = my_lev * share + (row & (share - 1))
    filled = jnp.zeros((2 * share, LANES), jnp.bool_)
    for t in range(cols):
        filled = filled | ((slot_in >= t * cap) & (slot_in < t * cap + jnp.minimum(count_ref[0, t], cap)))

    def mine(ref):
        whole = ref[...].astype(jnp.float32)
        part = whole[0:share]
        for j in range(1, levs):
            part = jnp.where(my_lev == j, whole[j * share : (j + 1) * share], part)
        return jnp.concatenate([part, part], axis=0)

    departure = jnp.where(
        filled & (mine(msk_ref) > 0.0), mine(wgt_ref) * (radiance - mine(val_ref)), 0.0
    )
    dep_in[my_lev] = departure
    dep_copies = send(4, "lev", lambda to: dep_in.at[my_lev], dep_in.at[my_lev])
    doubled = jnp.concatenate([departure, departure], axis=0).astype(jnp.bfloat16)
    spread_out = dot(doubled, jac_rows, 1)[0 : 2 * share]
    half = (row >= share) == ((my_lev & 1) == 1)
    for j in range(levs):
        part = jnp.where(own_lane, spread_out[:, j * LANES : (j + 1) * LANES], 0.0)
        amount = spread_groups(part, lev) * values[j]
        a_out[j] = jnp.where(half, amount, 0.0)
    a_in[my_id] = a_out[my_lev]
    a_copies = send(3, "all", lambda to: a_out.at[lax.rem(to, levs)], a_in.at[my_id])
    for copy in dep_copies:
        copy.wait()
    for j in range(levs):
        dep_ref[j * share : (j + 1) * share, :] = dep_in[j, 0:share, :]
    dep_store = pltpu.make_async_copy(dep_ref, dep_hbm, out_sem.at[out_sem.shape[0] - 1])
    dep_store.start()
    for copy in a_copies:
        copy.wait()
    for q in range(peers // 2):
        a_all[q * 2 * share : (q + 1) * 2 * share, :] = a_in[2 * q] + a_in[2 * q + 1]
    a_store = pltpu.make_async_copy(a_all, a_hbm, out_sem.at[1])
    a_store.start()
    for store in (wst_store, a_store, dep_store):
        store.wait()


def adjoint(
    cfg, ctl_hbm, cen_hbm, wst_hbm, a_hbm, dep_hbm, octl_hbm, ocen_hbm, odep_hbm,
    ctl, cen, wst, amount, dep, in_sem, out_sem,
):
    lev, cx, ny = cfg
    halves = range(ny // LANES)
    lanes_of = [slice(h * LANES, (h + 1) * LANES) for h in halves]
    pairs = [(a_hbm, amount), (wst_hbm, wst)]
    for h in halves:
        pairs += [(ctl_hbm.at[:, lanes_of[h]], ctl.at[h])]
        pairs += [(cen_hbm.at[e, :, lanes_of[h]], cen.at[e, h]) for e in range(2)]
    pairs += [(dep_hbm, dep)]
    loads = [pltpu.make_async_copy(src, dst, in_sem.at[i]) for i, (src, dst) in enumerate(pairs)]
    for load in loads:
        load.start()
    loads[0].wait()
    every = amount.shape[0]
    a_high, a_low = split(amount[...])
    a_high, a_low = a_high.astype(jnp.float32), a_low.astype(jnp.float32)
    left = jnp.concatenate([a_high, a_high, a_low, jnp.zeros_like(a_low)], axis=0).T
    left = left[:, 0 : 3 * every].astype(jnp.bfloat16)
    loads[1].wait()
    stores = []
    for h in halves:
        for load in loads[2 + 3 * h : 5 + 3 * h]:
            load.wait()
        for x in range(cx):
            pick = pl.ds(x, lev, stride=cx)
            add = dot(left, wst[x, :, lanes_of[h]], 0)
            for i, ref in enumerate((ctl.at[h], cen.at[0, h], cen.at[1, h])):
                ref[pick, :] = ref[pick, :] + add[i * lev : (i + 1) * lev]
        pairs = [(ctl.at[h], octl_hbm.at[:, lanes_of[h]])]
        pairs += [(cen.at[e, h], ocen_hbm.at[e, :, lanes_of[h]]) for e in range(2)]
        for src, dst in pairs:
            stores.append(pltpu.make_async_copy(src, dst, out_sem.at[len(stores)]))
            stores[-1].start()
    loads[-1].wait()
    stores.append(pltpu.make_async_copy(dep, odep_hbm, out_sem.at[len(stores)]))
    stores[-1].start()
    for store in stores:
        store.wait()


def fits(members, levels, cells_x, cells_y, slot_total, channels, peers, level_blocks):
    def power(n):
        return n & (n - 1) == 0
    return (
        members == 2 and levels * 4 == LANES and channels == LANES and cells_x == 8
        and cells_y % LANES == 0 and power(cells_y) and cells_y <= 256 and power(peers) and slot_total % 16 == 0
        and power(slot_total // peers) and peers * slot_total * 3 <= 256
        and peers * cells_x > 2 * STEPS and slot_total == 4 * level_blocks and level_blocks == 4
    )


def local_fused(control, control_ens, ensemble, spread, jacobian, obs_value, obs_weight, channel_mask, obs_cell, obs_count):
    members = control_ens.shape[0]
    levels, cells_x, cells_y = control.shape
    slots, _, channels = jacobian.shape
    cols, levs = lax.axis_size("col"), lax.axis_size("lev")
    every, peers, share = cols * slots, cols * levs, slots // levs
    flat = (levels * cells_x, cells_y)
    cut = (cells_y // LANES, levels * cells_x, LANES)
    hbm = pl.BlockSpec(memory_space=pltpu.HBM)
    weights, amount, held = pl.pallas_call(
        functools.partial(fused, (cols, levs, slots, levels, cells_x, cells_y)),
        out_shape=(
            jax.ShapeDtypeStruct((cells_x, 3 * every, cells_y), jnp.bfloat16),
            jax.ShapeDtypeStruct((every, LANES), jnp.float32),
            jax.ShapeDtypeStruct((slots, channels), jnp.float32),
        ),
        in_specs=[hbm] * 10,
        out_specs=(hbm, hbm, hbm),
        scratch_shapes=[
            pltpu.VMEM(cut, jnp.float32),
            pltpu.VMEM((members,) + cut, jnp.float32),
            pltpu.VMEM(ensemble.shape, jnp.bfloat16),
            pltpu.VMEM((members,) + cut, jnp.float32),
            pltpu.VMEM(cut, jnp.float32),
            pltpu.VMEM((levs, share) + jacobian.shape[1:], jnp.bfloat16),
            pltpu.VMEM(obs_value.shape, jnp.bfloat16),
            pltpu.VMEM(obs_weight.shape, jnp.bfloat16),
            pltpu.VMEM(channel_mask.shape, jnp.int32),
            pltpu.SMEM(obs_cell.shape, jnp.int32),
            pltpu.SMEM(obs_count.shape, jnp.int32),
            pltpu.VMEM((every, LANES), jnp.int32),
            pltpu.VMEM((slots, channels), jnp.float32),
            pltpu.VMEM((STEPS + 1, every, cells_y), jnp.float32),
            pltpu.VMEM((cells_x, 2 * LANES, cells_y), jnp.bfloat16),
            pltpu.VMEM((cells_x, LANES, cells_y), jnp.bfloat16),
            pltpu.VMEM((cells_x, 3 * every, cells_y), jnp.bfloat16),
            pltpu.VMEM((peers, 2 * share, LANES), jnp.float32),
            pltpu.VMEM((peers, 2 * share, LANES), jnp.float32),
            pltpu.VMEM((levs, 2 * share, LANES), jnp.float32),
            pltpu.VMEM((levs, 2 * share, LANES), jnp.float32),
            pltpu.VMEM((peers, 2 * share, LANES), jnp.float32),
            pltpu.VMEM((every, LANES), jnp.float32),
            pltpu.SemaphoreType.DMA((7 + (members + 2) * cut[0],)),
            pltpu.SemaphoreType.DMA((3,)),
            pltpu.SemaphoreType.DMA((5, peers)),
            pltpu.SemaphoreType.DMA((5, peers)),
        ],
        compiler_params=pltpu.CompilerParams(
            collective_id=0, has_side_effects=True, vmem_limit_bytes=63 * 1024 * 1024
        ),
    )(
        control.reshape(flat), control_ens.reshape((members,) + flat), ensemble, spread.reshape(flat),
        jacobian, obs_value, obs_weight, channel_mask, obs_cell, obs_count,
    )
    out_control, out_ens, departures = pl.pallas_call(
        functools.partial(adjoint, (levels, cells_x, cells_y)),
        out_shape=(
            jax.ShapeDtypeStruct(flat, jnp.float32),
            jax.ShapeDtypeStruct((members,) + flat, jnp.float32),
            jax.ShapeDtypeStruct((slots, channels), jnp.float32),
        ),
        in_specs=[hbm] * 5,
        out_specs=(hbm,) * 3,
        scratch_shapes=[
            pltpu.VMEM(cut, jnp.float32),
            pltpu.VMEM((members,) + cut, jnp.float32),
            pltpu.VMEM((cells_x, 3 * every, cells_y), jnp.bfloat16),
            pltpu.VMEM((every, LANES), jnp.float32),
            pltpu.VMEM((slots, channels), jnp.float32),
            pltpu.SemaphoreType.DMA((3 + (members + 1) * cut[0],)),
            pltpu.SemaphoreType.DMA((1 + (members + 1) * cut[0],)),
        ],
        compiler_params=pltpu.CompilerParams(vmem_limit_bytes=63 * 1024 * 1024),
    )(control.reshape(flat), control_ens.reshape((members,) + flat), weights, amount, held)
    return out_control.reshape(control.shape), out_ens.reshape(control_ens.shape), departures


def pick_local(control, control_ens, ensemble, spread, jacobian, *obs):
    sizes = (control_ens.shape[0],) + control.shape + (jacobian.shape[0], jacobian.shape[2], lax.axis_size("col"), lax.axis_size("lev"))
    run = local_fused if fits(*sizes) else local
    return run(control, control_ens, ensemble, spread, jacobian, *obs)


def solution(mesh):
    placed = (
        P(("grp", "lev"), "col", None),
        P("grp", "lev", "col", None),
        P("grp", "lev", "col", None),
        P(("grp", "lev"), "col", None),
        P(("grp", "col"), "lev", None),
        P(("grp", "col"), None),
        P(("grp", "col"), None),
        P(("grp", "col"), None),
        P(("grp", "col")),
        P(("grp", "col"), None),
    )
    return jax.shard_map(
        pick_local,
        mesh=mesh,
        in_specs=placed,
        out_specs=(
            P(("grp", "lev"), "col", None),
            P("grp", "lev", "col", None),
            P(("grp", "col"), None),
        ),
        check_vma=False,
    )
```

```python
import math

import jax
import jax.numpy as jnp
from jax import lax
from jax.experimental import pallas as pl
from jax.experimental.pallas import tpu as pltpu
from jax.sharding import PartitionSpec as P
import functools
import numpy as np

STEPS = 4


rate_x = 0.35
rate_y = 0.1


def padded_2(value, sides, width):
    for axis, dim in sides:
        peers, length = (lax.axis_size(axis), value.shape[dim])
        up = [(i, (i + 1) % peers) for i in range(peers)]
        down = [(j, i) for i, j in up]
        last = lax.slice_in_dim(value, length - width, length, axis=dim)
        initial = lax.slice_in_dim(value, 0, width, axis=dim)
        before = lax.ppermute(last, axis, up)
        after = lax.ppermute(initial, axis, down)
        value = jnp.concatenate([before, value, after], axis=dim)
    return value


def smooth(fields):
    for iteration in range(STEPS):
        padded = padded_2(fields, (("col", 2),), 1)
        beside = jnp.pad(fields, ((0, 0), (0, 0), (0, 0), (1, 1)))
        along_x = padded[:, :, 2:, :] + padded[:, :, :-2, :] - 2.0 * fields
        along_y = beside[..., 2:] + beside[..., :-2] - 2.0 * fields
        fields = fields + rate_x * along_x + rate_y * along_y
    return fields


def solve_rows(jac_rows, columns, values, weights, masks, filled):
    partial_value = jnp.einsum("rlc,rl->rc", jac_rows, columns, preferred_element_type=jnp.float32)
    radiance = lax.psum(partial_value, "lev")
    active = (filled[:, None] > 0) & (masks > 0)
    departure = jnp.where(
        active, weights.astype(jnp.float32) * (radiance - values.astype(jnp.float32)), 0.0
    )
    increment = jnp.einsum(
        "rc,rlc->rl", departure.astype(jnp.bfloat16), jac_rows, preferred_element_type=jnp.float32
    )
    return (departure, increment)


def local(
    control,
    control_ens,
    ensemble,
    spread,
    jacobian,
    obs_value,
    obs_weight,
    channel_mask,
    obs_cell,
    obs_count,
):
    members = control_ens.shape[0]
    ens_scale = 1.0 / math.sqrt(members)
    levels, cells_x, cells_y = control.shape
    peer_count = lax.axis_size("col")
    slot_total = jacobian.shape[0]
    capacity = slot_total // peer_count
    smoothed = smooth(jnp.concatenate([control[None], control_ens], 0))
    analysis = spread * smoothed[0] + jnp.sum(ensemble * smoothed[1:], 0) * ens_scale
    flat_state = analysis.reshape(levels, cells_x * cells_y)
    row_ids = jnp.arange(slot_total, dtype=jnp.int32)
    target = row_ids // capacity
    slot_index = row_ids % capacity
    filled = (slot_index < obs_count[0][target]).astype(jnp.int32)
    empty_grid = jnp.zeros((levels, cells_x * cells_y), jnp.float32)
    jac_recv, value_recv, weight_recv, mask_recv, cell_recv, filled_recv = (
        lax.all_to_all(jacobian, "col", split_axis=0, concat_axis=0, tiled=True),
        lax.all_to_all(obs_value, "col", split_axis=0, concat_axis=0, tiled=True),
        lax.all_to_all(obs_weight, "col", split_axis=0, concat_axis=0, tiled=True),
        lax.all_to_all(channel_mask, "col", split_axis=0, concat_axis=0, tiled=True),
        lax.all_to_all(obs_cell, "col", split_axis=0, concat_axis=0, tiled=True),
        lax.all_to_all(filled, "col", split_axis=0, concat_axis=0, tiled=True),
    )
    columns = flat_state[:, cell_recv].T.astype(jnp.bfloat16)
    departure, increment = solve_rows(
        jac_recv, columns, value_recv, weight_recv, mask_recv, filled_recv
    )
    gradient_flat = empty_grid.at[:, cell_recv].add(increment.T)
    departures = lax.all_to_all(departure, "col", split_axis=0, concat_axis=0, tiled=True)
    gradient_field = gradient_flat.reshape(levels, cells_x, cells_y)
    adjoint = smooth(
        jnp.concatenate(
            [(spread * gradient_field)[None], ensemble * gradient_field[None] * ens_scale], 0
        )
    )
    return (control + adjoint[0], control_ens + adjoint[1:], departures)


LANES = 128


def stencil_power():
    step = np.array([[0.0, rate_x, 0.0], [rate_y, 1.0 - 2.0 * rate_x - 2.0 * rate_y, rate_y], [0.0, rate_x, 0.0]])
    total = np.zeros((2 * STEPS + 1, 2 * STEPS + 1))
    total[STEPS, STEPS] = 1.0
    for _ in range(STEPS):
        wide = np.pad(total, 1)
        total = sum(
            step[i, j] * wide[i : i + 2 * STEPS + 1, j : j + 2 * STEPS + 1]
            for i in range(3)
            for j in range(3)
        )
    return total[STEPS:, STEPS:]


def split(value):
    high = value.astype(jnp.bfloat16)
    return high, (value - high.astype(jnp.float32)).astype(jnp.bfloat16)


def dot(a, b, b_dim):
    return lax.dot_general(a, b, (((1,), (b_dim,)), ((), ())), preferred_element_type=jnp.float32)


def spread_groups(value, width):
    total = value
    for shift in range(width, LANES, width):
        total = total + pltpu.roll(value, shift, 1)
    return total


def fused(
    cfg,
    ctl_hbm, cen_hbm, ens_hbm, spr_hbm, jac_hbm, val_hbm, wgt_hbm, msk_hbm, cell_hbm, count_hbm,
    wst_hbm, a_hbm, dep_hbm,
    ctl, cen, ens, ensf, spr, jac, val_ref, wgt_ref, msk_ref, cell_ref, count_ref, cells, dep_ref, ey, fst, vst, wst, pv, pv_in, dep_in, a_out, a_in, a_all,
    in_sem, out_sem, send_sem, recv_sem,
):
    cols, levs, slots, lev, cx, ny = cfg
    cap = slots // cols
    nx = cols * cx
    every = cols * slots
    me, my_lev = lax.axis_index("col"), lax.axis_index("lev")
    table = stencil_power()

    halves = range(ny // LANES)
    lanes_of = [slice(h * LANES, (h + 1) * LANES) for h in halves]
    pairs = [(ctl_hbm.at[:, lanes_of[h]], ctl.at[h]) for h in halves]
    pairs += [(cen_hbm.at[e, :, lanes_of[h]], cen.at[e, h]) for e in range(2) for h in halves]
    fields = len(pairs)
    pairs += [(ens_hbm, ens)] + [(spr_hbm.at[:, lanes_of[h]], spr.at[h]) for h in halves]
    small = len(pairs)
    pairs += [(jac_hbm.at[pl.ds(my_lev * (slots // levs), slots // levs)], jac.at[my_lev]), (val_hbm, val_ref), (wgt_hbm, wgt_ref), (msk_hbm, msk_ref), (count_hbm, count_ref)]
    pairs += [(cell_hbm, cell_ref)]
    loads = [pltpu.make_async_copy(src, dst, in_sem.at[i]) for i, (src, dst) in enumerate(pairs)]
    loads[-1].start()
    barrier = pltpu.get_barrier_semaphore()
    peers = cols * levs
    my_id = me * levs + my_lev
    for axis, count, mine in (("col", cols, me), ("lev", levs, my_lev)):
        for d in range(1, count):
            pl.semaphore_signal(
                barrier, inc=1, device_id={axis: lax.rem(mine + d, count)}, device_id_type=pl.DeviceIdType.MESH
            )
    for load in loads[:-1]:
        load.start()

    def send(phase, axis, src_of, dst):
        count, mine = {"col": (cols, me), "lev": (levs, my_lev), "all": (peers, my_id)}[axis]
        copies = []
        for d in range(1, count):
            to = lax.rem(mine + d, count)
            device = {"col": lax.div(to, levs), "lev": lax.rem(to, levs)} if axis == "all" else {axis: to}
            copy = pltpu.make_async_remote_copy(
                src_ref=src_of(to),
                dst_ref=dst,
                send_sem=send_sem.at[phase, d],
                recv_sem=recv_sem.at[phase, d],
                device_id=device,
                device_id_type=pl.DeviceIdType.MESH,
            )
            copy.start()
            copies.append(copy)
        return copies

    loads[-1].wait()
    row = lax.broadcasted_iota(jnp.int32, (slots, LANES), 0)
    lane = lax.broadcasted_iota(jnp.int32, (slots, LANES), 1)
    own = jnp.zeros((slots, LANES), jnp.int32)
    for r in range(slots):
        own = jnp.where(row == r, cell_ref[r], own)
    my_rows = pl.ds(pl.multiple_of(me * slots, slots), slots)
    cells[my_rows, :] = own
    pl.semaphore_wait(barrier, cols + levs - 2)
    cell_copies = send(0, "col", lambda to: cells.at[my_rows], cells.at[my_rows])
    share = slots // levs
    jac_copies = send(2, "lev", lambda to: jac_hbm.at[pl.ds(to * share, share)], jac.at[my_lev])

    for load in loads[:fields]:
        load.wait()
    zeros = jnp.zeros((lev, ny), jnp.bfloat16)
    picks = [pl.ds(x, lev, stride=cx) for x in range(cx)]
    for x in range(cx):
        for i, ref in enumerate((ctl, cen.at[0], cen.at[1])):
            for h in halves:
                high, low = split(ref.at[h][picks[x], :])
                fst[x, i * lev : (i + 1) * lev, lanes_of[h]] = high
                fst[x, LANES + i * lev : LANES + (i + 1) * lev, lanes_of[h]] = low
        fst[x, 3 * lev : 4 * lev, :] = zeros
        fst[x, LANES + 3 * lev : LANES + 4 * lev, :] = zeros
    for load in loads[fields:small]:
        load.wait()
    for e in range(2):
        member = ens[e].astype(jnp.float32).reshape(lev * cx, ny)
        for h in halves:
            ensf[e, h] = member[:, lanes_of[h]]
    for x in range(cx):
        for h in halves:
            high, low = split(spr.at[h][picks[x], :])
            vst[x, 0:lev, lanes_of[h]] = high
            vst[x, lev : 2 * lev, lanes_of[h]] = ensf.at[0, h][picks[x], :].astype(jnp.bfloat16)
            vst[x, 2 * lev : 3 * lev, lanes_of[h]] = ensf.at[1, h][picks[x], :].astype(jnp.bfloat16)
            vst[x, 3 * lev : 4 * lev, lanes_of[h]] = low

    for copy in cell_copies:
        copy.wait()

    cell = cells[...]
    shift = ny.bit_length() - 1
    cell_x = lax.shift_right_logical(cell, jnp.full_like(cell, shift))
    cell_y = cell & (ny - 1)
    slot = lax.broadcasted_iota(jnp.int32, (every, LANES), 0)
    target = lax.shift_right_logical(slot, jnp.full_like(slot, cap.bit_length() - 1)) & (cols - 1)
    apart = me * cx - (target * cx + cell_x)
    y_lane = lax.broadcasted_iota(jnp.int32, (every, LANES), 1)
    for h in range(ny // LANES):
        y = y_lane + h * LANES
        dy = jnp.abs(y - cell_y)
        below = y + cell_y + 2
        above = 2 * ny - y - cell_y
        for m in range(STEPS + 1):
            one = jnp.where(dy == m, 1.0, 0.0)
            if m >= 2:
                one = one - jnp.where((below == m) | (above == m), 1.0, 0.0)
            ey[m, :, h * LANES : (h + 1) * LANES] = one
    out = None
    for x in range(cx):
        dx = apart + x
        dx = jnp.where(dx >= nx // 2, dx - nx, dx)
        dx = jnp.abs(jnp.where(dx < -(nx // 2), dx + nx, dx))
        at = [dx == q for q in range(STEPS + 1)]
        factors = []
        for m in range(STEPS + 1):
            factor = jnp.zeros((every, LANES), jnp.float32)
            for q in range(STEPS + 1 - m):
                factor = jnp.where(at[q], float(table[q, m]), factor)
            factors.append(factor)
        here = jnp.where(at[0], 1.0, 0.0)
        hits = []
        for h in range(ny // LANES):
            part = slice(h * LANES, (h + 1) * LANES)
            centre = ey[0, :, part]
            weight = factors[0] * centre
            for m in range(1, STEPS + 1):
                weight = weight + factors[m] * ey[m, :, part]
            high, low = split(weight)
            wst[x, 0:every, part] = high
            wst[x, every : 2 * every, part] = low
            wst[x, 2 * every : 3 * every, part] = high
            hits.append((here * centre).astype(jnp.bfloat16))
        sums = dot(wst[x, 0 : 2 * every, :], fst[x], 1)
        found = dot(jnp.concatenate(hits, axis=1), vst[x], 1)
        out = (sums, found) if out is None else (out[0] + sums, out[1] + found)
    sums, found = out
    wst_store = pltpu.make_async_copy(wst, wst_hbm, out_sem.at[0])
    wst_store.start()
    sums = sums[0:every, 0:LANES] + sums[0:every, LANES:] + sums[every:, 0:LANES]
    group = lax.shift_right_logical(y_lane, jnp.full_like(y_lane, lev.bit_length() - 1))
    found = jnp.where(group == 0, found + pltpu.roll(found, lev, 1), found * (1.0 / math.sqrt(2)))
    found = jnp.where(group == 3, 0.0, found)
    for q in range(peers):
        pv[q, 0:share, :] = sums[q * share : (q + 1) * share]
        pv[q, share:, :] = found[q * share : (q + 1) * share]
    pv_in[my_id] = pv[my_id]
    copies = send(1, "all", lambda to: pv.at[to], pv_in.at[my_id])
    for load in loads[small:-1]:
        load.wait()
    for copy in jac_copies + copies:
        copy.wait()

    row = lax.broadcasted_iota(jnp.int32, (2 * share, LANES), 0)
    lane = lax.broadcasted_iota(jnp.int32, (2 * share, LANES), 1)
    own_lane = lax.shift_right_logical(lane, jnp.full_like(lane, lev.bit_length() - 1)) == (row & (share - 1))
    values, blocks = [], []
    for j in range(levs):
        both = pv_in[j]
        for s in range(1, cols):
            both = both + pv_in[s * levs + j]
        turned = pltpu.roll(both, share, 0)
        values.append(jnp.where(row < share, turned, both))
        blocks.append(jnp.where(own_lane, spread_groups(both * turned, lev), 0.0))
    jac_rows = jac[...].reshape(slots * lev, LANES)
    block = jnp.concatenate([jnp.concatenate(blocks, axis=1)] * 2, axis=0).astype(jnp.bfloat16)
    radiance = dot(block, jac_rows, 0)[0 : 2 * share]

    slot_in = my_lev * share + (row & (share - 1))
    filled = jnp.zeros((2 * share, LANES), jnp.bool_)
    for t in range(cols):
        filled = filled | ((slot_in >= t * cap) & (slot_in < t * cap + jnp.minimum(count_ref[0, t], cap)))

    def mine(ref):
        whole = ref[...].astype(jnp.float32)
        part = whole[0:share]
        for j in range(1, levs):
            part = jnp.where(my_lev == j, whole[j * share : (j + 1) * share], part)
        return jnp.concatenate([part, part], axis=0)

    departure = jnp.where(
        filled & (mine(msk_ref) > 0.0), mine(wgt_ref) * (radiance - mine(val_ref)), 0.0
    )
    dep_in[my_lev] = departure
    dep_copies = send(4, "lev", lambda to: dep_in.at[my_lev], dep_in.at[my_lev])
    doubled = jnp.concatenate([departure, departure], axis=0).astype(jnp.bfloat16)
    spread_out = dot(doubled, jac_rows, 1)[0 : 2 * share]
    half = (row >= share) == ((my_lev & 1) == 1)
    for j in range(levs):
        part = jnp.where(own_lane, spread_out[:, j * LANES : (j + 1) * LANES], 0.0)
        amount = spread_groups(part, lev) * values[j]
        a_out[j] = jnp.where(half, amount, 0.0)
    a_in[my_id] = a_out[my_lev]
    a_copies = send(3, "all", lambda to: a_out.at[lax.rem(to, levs)], a_in.at[my_id])
    for copy in dep_copies:
        copy.wait()
    for j in range(levs):
        dep_ref[j * share : (j + 1) * share, :] = dep_in[j, 0:share, :]
    dep_store = pltpu.make_async_copy(dep_ref, dep_hbm, out_sem.at[out_sem.shape[0] - 1])
    dep_store.start()
    for copy in a_copies:
        copy.wait()
    for q in range(peers // 2):
        a_all[q * 2 * share : (q + 1) * 2 * share, :] = a_in[2 * q] + a_in[2 * q + 1]
    a_store = pltpu.make_async_copy(a_all, a_hbm, out_sem.at[1])
    a_store.start()
    for store in (wst_store, a_store, dep_store):
        store.wait()


def adjoint(
    cfg, ctl_hbm, cen_hbm, wst_hbm, a_hbm, dep_hbm, octl_hbm, ocen_hbm, odep_hbm,
    ctl, cen, wst, amount, dep, in_sem, out_sem,
):
    lev, cx, ny = cfg
    halves = range(ny // LANES)
    lanes_of = [slice(h * LANES, (h + 1) * LANES) for h in halves]
    pairs = [(a_hbm, amount), (wst_hbm, wst)]
    for h in halves:
        pairs += [(ctl_hbm.at[:, lanes_of[h]], ctl.at[h])]
        pairs += [(cen_hbm.at[e, :, lanes_of[h]], cen.at[e, h]) for e in range(2)]
    pairs += [(dep_hbm, dep)]
    loads = [pltpu.make_async_copy(src, dst, in_sem.at[i]) for i, (src, dst) in enumerate(pairs)]
    for load in loads:
        load.start()
    loads[0].wait()
    every = amount.shape[0]
    a_high, a_low = split(amount[...])
    a_high, a_low = a_high.astype(jnp.float32), a_low.astype(jnp.float32)
    left = jnp.concatenate([a_high, a_high, a_low, jnp.zeros_like(a_low)], axis=0).T
    left = left[:, 0 : 3 * every].astype(jnp.bfloat16)
    loads[1].wait()
    stores = []
    for h in halves:
        for load in loads[2 + 3 * h : 5 + 3 * h]:
            load.wait()
        for x in range(cx):
            pick = pl.ds(x, lev, stride=cx)
            add = dot(left, wst[x, :, lanes_of[h]], 0)
            for i, ref in enumerate((ctl.at[h], cen.at[0, h], cen.at[1, h])):
                ref[pick, :] = ref[pick, :] + add[i * lev : (i + 1) * lev]
        pairs = [(ctl.at[h], octl_hbm.at[:, lanes_of[h]])]
        pairs += [(cen.at[e, h], ocen_hbm.at[e, :, lanes_of[h]]) for e in range(2)]
        for src, dst in pairs:
            stores.append(pltpu.make_async_copy(src, dst, out_sem.at[len(stores)]))
            stores[-1].start()
    loads[-1].wait()
    stores.append(pltpu.make_async_copy(dep, odep_hbm, out_sem.at[len(stores)]))
    stores[-1].start()
    for store in stores:
        store.wait()


def fits(members, levels, cells_x, cells_y, slot_total, channels, peers, level_blocks):
    def power(n):
        return n & (n - 1) == 0
    return (
        members == 2 and levels * 4 == LANES and channels == LANES and cells_x == 8
        and cells_y % LANES == 0 and power(cells_y) and cells_y <= 256 and power(peers) and slot_total % 16 == 0
        and power(slot_total // peers) and peers * slot_total * 3 <= 256
        and peers * cells_x > 2 * STEPS and slot_total == 4 * level_blocks and level_blocks == 4
    )


def local_fused(control, control_ens, ensemble, spread, jacobian, obs_value, obs_weight, channel_mask, obs_cell, obs_count):
    members = control_ens.shape[0]
    levels, cells_x, cells_y = control.shape
    slots, _, channels = jacobian.shape
    cols, levs = lax.axis_size("col"), lax.axis_size("lev")
    every, peers, share = cols * slots, cols * levs, slots // levs
    flat = (levels * cells_x, cells_y)
    cut = (cells_y // LANES, levels * cells_x, LANES)
    hbm = pl.BlockSpec(memory_space=pltpu.HBM)
    weights, amount, held = pl.pallas_call(
        functools.partial(fused, (cols, levs, slots, levels, cells_x, cells_y)),
        out_shape=(
            jax.ShapeDtypeStruct((cells_x, 3 * every, cells_y), jnp.bfloat16),
            jax.ShapeDtypeStruct((every, LANES), jnp.float32),
            jax.ShapeDtypeStruct((slots, channels), jnp.float32),
        ),
        in_specs=[hbm] * 10,
        out_specs=(hbm, hbm, hbm),
        scratch_shapes=[
            pltpu.VMEM(cut, jnp.float32),
            pltpu.VMEM((members,) + cut, jnp.float32),
            pltpu.VMEM(ensemble.shape, jnp.bfloat16),
            pltpu.VMEM((members,) + cut, jnp.float32),
            pltpu.VMEM(cut, jnp.float32),
            pltpu.VMEM((levs, share) + jacobian.shape[1:], jnp.bfloat16),
            pltpu.VMEM(obs_value.shape, jnp.bfloat16),
            pltpu.VMEM(obs_weight.shape, jnp.bfloat16),
            pltpu.VMEM(channel_mask.shape, jnp.int32),
            pltpu.SMEM(obs_cell.shape, jnp.int32),
            pltpu.SMEM(obs_count.shape, jnp.int32),
            pltpu.VMEM((every, LANES), jnp.int32),
            pltpu.VMEM((slots, channels), jnp.float32),
            pltpu.VMEM((STEPS + 1, every, cells_y), jnp.float32),
            pltpu.VMEM((cells_x, 2 * LANES, cells_y), jnp.bfloat16),
            pltpu.VMEM((cells_x, LANES, cells_y), jnp.bfloat16),
            pltpu.VMEM((cells_x, 3 * every, cells_y), jnp.bfloat16),
            pltpu.VMEM((peers, 2 * share, LANES), jnp.float32),
            pltpu.VMEM((peers, 2 * share, LANES), jnp.float32),
            pltpu.VMEM((levs, 2 * share, LANES), jnp.float32),
            pltpu.VMEM((levs, 2 * share, LANES), jnp.float32),
            pltpu.VMEM((peers, 2 * share, LANES), jnp.float32),
            pltpu.VMEM((every, LANES), jnp.float32),
            pltpu.SemaphoreType.DMA((7 + (members + 2) * cut[0],)),
            pltpu.SemaphoreType.DMA((3,)),
            pltpu.SemaphoreType.DMA((5, peers)),
            pltpu.SemaphoreType.DMA((5, peers)),
        ],
        compiler_params=pltpu.CompilerParams(
            collective_id=0, has_side_effects=True, vmem_limit_bytes=63 * 1024 * 1024
        ),
    )(
        control.reshape(flat), control_ens.reshape((members,) + flat), ensemble, spread.reshape(flat),
        jacobian, obs_value, obs_weight, channel_mask, obs_cell, obs_count,
    )
    out_control, out_ens, departures = pl.pallas_call(
        functools.partial(adjoint, (levels, cells_x, cells_y)),
        out_shape=(
            jax.ShapeDtypeStruct(flat, jnp.float32),
            jax.ShapeDtypeStruct((members,) + flat, jnp.float32),
            jax.ShapeDtypeStruct((slots, channels), jnp.float32),
        ),
        in_specs=[hbm] * 5,
        out_specs=(hbm,) * 3,
        scratch_shapes=[
            pltpu.VMEM(cut, jnp.float32),
            pltpu.VMEM((members,) + cut, jnp.float32),
            pltpu.VMEM((cells_x, 3 * every, cells_y), jnp.bfloat16),
            pltpu.VMEM((every, LANES), jnp.float32),
            pltpu.VMEM((slots, channels), jnp.float32),
            pltpu.SemaphoreType.DMA((3 + (members + 1) * cut[0],)),
            pltpu.SemaphoreType.DMA((1 + (members + 1) * cut[0],)),
        ],
        compiler_params=pltpu.CompilerParams(vmem_limit_bytes=63 * 1024 * 1024),
    )(control.reshape(flat), control_ens.reshape((members,) + flat), weights, amount, held)
    return out_control.reshape(control.shape), out_ens.reshape(control_ens.shape), departures


def pick_local(control, control_ens, ensemble, spread, jacobian, *obs):
    sizes = (control_ens.shape[0],) + control.shape + (jacobian.shape[0], jacobian.shape[2], lax.axis_size("col"), lax.axis_size("lev"))
    run = local_fused if fits(*sizes) else local
    return run(control, control_ens, ensemble, spread, jacobian, *obs)


def solution(mesh):
    placed = (
        P(("grp", "lev"), "col", None),
        P("grp", "lev", "col", None),
        P("grp", "lev", "col", None),
        P(("grp", "lev"), "col", None),
        P(("grp", "col"), "lev", None),
        P(("grp", "col"), None),
        P(("grp", "col"), None),
        P(("grp", "col"), None),
        P(("grp", "col")),
        P(("grp", "col"), None),
    )
    return jax.shard_map(
        pick_local,
        mesh=mesh,
        in_specs=placed,
        out_specs=(
            P(("grp", "lev"), "col", None),
            P("grp", "lev", "col", None),
            P(("grp", "col"), None),
        ),
        check_vma=False,
    )
```

```python
import math

import jax
import jax.numpy as jnp
from jax import lax
from jax.experimental import pallas as pl
from jax.experimental.pallas import tpu as pltpu
from jax.sharding import PartitionSpec as P
import functools
import numpy as np

STEPS = 4


rate_x = 0.35
rate_y = 0.1


def padded_2(value, sides, width):
    for axis, dim in sides:
        peers, length = (lax.axis_size(axis), value.shape[dim])
        up = [(i, (i + 1) % peers) for i in range(peers)]
        down = [(j, i) for i, j in up]
        last = lax.slice_in_dim(value, length - width, length, axis=dim)
        initial = lax.slice_in_dim(value, 0, width, axis=dim)
        before = lax.ppermute(last, axis, up)
        after = lax.ppermute(initial, axis, down)
        value = jnp.concatenate([before, value, after], axis=dim)
    return value


def smooth(fields):
    for iteration in range(STEPS):
        padded = padded_2(fields, (("col", 2),), 1)
        beside = jnp.pad(fields, ((0, 0), (0, 0), (0, 0), (1, 1)))
        along_x = padded[:, :, 2:, :] + padded[:, :, :-2, :] - 2.0 * fields
        along_y = beside[..., 2:] + beside[..., :-2] - 2.0 * fields
        fields = fields + rate_x * along_x + rate_y * along_y
    return fields


def solve_rows(jac_rows, columns, values, weights, masks, filled):
    partial_value = jnp.einsum("rlc,rl->rc", jac_rows, columns, preferred_element_type=jnp.float32)
    radiance = lax.psum(partial_value, "lev")
    active = (filled[:, None] > 0) & (masks > 0)
    departure = jnp.where(
        active, weights.astype(jnp.float32) * (radiance - values.astype(jnp.float32)), 0.0
    )
    increment = jnp.einsum(
        "rc,rlc->rl", departure.astype(jnp.bfloat16), jac_rows, preferred_element_type=jnp.float32
    )
    return (departure, increment)


def local(
    control,
    control_ens,
    ensemble,
    spread,
    jacobian,
    obs_value,
    obs_weight,
    channel_mask,
    obs_cell,
    obs_count,
):
    members = control_ens.shape[0]
    ens_scale = 1.0 / math.sqrt(members)
    levels, cells_x, cells_y = control.shape
    peer_count = lax.axis_size("col")
    slot_total = jacobian.shape[0]
    capacity = slot_total // peer_count
    smoothed = smooth(jnp.concatenate([control[None], control_ens], 0))
    analysis = spread * smoothed[0] + jnp.sum(ensemble * smoothed[1:], 0) * ens_scale
    flat_state = analysis.reshape(levels, cells_x * cells_y)
    row_ids = jnp.arange(slot_total, dtype=jnp.int32)
    target = row_ids // capacity
    slot_index = row_ids % capacity
    filled = (slot_index < obs_count[0][target]).astype(jnp.int32)
    empty_grid = jnp.zeros((levels, cells_x * cells_y), jnp.float32)
    jac_recv, value_recv, weight_recv, mask_recv, cell_recv, filled_recv = (
        lax.all_to_all(jacobian, "col", split_axis=0, concat_axis=0, tiled=True),
        lax.all_to_all(obs_value, "col", split_axis=0, concat_axis=0, tiled=True),
        lax.all_to_all(obs_weight, "col", split_axis=0, concat_axis=0, tiled=True),
        lax.all_to_all(channel_mask, "col", split_axis=0, concat_axis=0, tiled=True),
        lax.all_to_all(obs_cell, "col", split_axis=0, concat_axis=0, tiled=True),
        lax.all_to_all(filled, "col", split_axis=0, concat_axis=0, tiled=True),
    )
    columns = flat_state[:, cell_recv].T.astype(jnp.bfloat16)
    departure, increment = solve_rows(
        jac_recv, columns, value_recv, weight_recv, mask_recv, filled_recv
    )
    gradient_flat = empty_grid.at[:, cell_recv].add(increment.T)
    departures = lax.all_to_all(departure, "col", split_axis=0, concat_axis=0, tiled=True)
    gradient_field = gradient_flat.reshape(levels, cells_x, cells_y)
    adjoint = smooth(
        jnp.concatenate(
            [(spread * gradient_field)[None], ensemble * gradient_field[None] * ens_scale], 0
        )
    )
    return (control + adjoint[0], control_ens + adjoint[1:], departures)


LANES = 128


def stencil_power():
    step = np.array([[0.0, rate_x, 0.0], [rate_y, 1.0 - 2.0 * rate_x - 2.0 * rate_y, rate_y], [0.0, rate_x, 0.0]])
    total = np.zeros((2 * STEPS + 1, 2 * STEPS + 1))
    total[STEPS, STEPS] = 1.0
    for _ in range(STEPS):
        wide = np.pad(total, 1)
        total = sum(
            step[i, j] * wide[i : i + 2 * STEPS + 1, j : j + 2 * STEPS + 1]
            for i in range(3)
            for j in range(3)
        )
    return total[STEPS:, STEPS:]


def split(value):
    high = value.astype(jnp.bfloat16)
    return high, (value - high.astype(jnp.float32)).astype(jnp.bfloat16)


def dot(a, b, b_dim):
    return lax.dot_general(a, b, (((1,), (b_dim,)), ((), ())), preferred_element_type=jnp.float32)


def spread_groups(value, width):
    total = value
    for shift in range(width, LANES, width):
        total = total + pltpu.roll(value, shift, 1)
    return total


def fused(
    cfg,
    ctl_hbm, cen_hbm, ens_hbm, spr_hbm, jac_hbm, val_hbm, wgt_hbm, msk_hbm, cell_hbm, count_hbm,
    wst_hbm, a_hbm, dep_hbm,
    ctl, cen, ens, ensf, spr, jac, val_ref, wgt_ref, msk_ref, cell_ref, count_ref, cells, dep_ref, ey, fst, vst, wst, pv, pv_in, dep_in, a_out, a_in, a_all,
    in_sem, out_sem, send_sem, recv_sem,
):
    cols, levs, slots, lev, cx, ny = cfg
    cap = slots // cols
    nx = cols * cx
    every = cols * slots
    me, my_lev = lax.axis_index("col"), lax.axis_index("lev")
    table = stencil_power()

    halves = range(ny // LANES)
    lanes_of = [slice(h * LANES, (h + 1) * LANES) for h in halves]
    pairs = [(ctl_hbm.at[:, lanes_of[h]], ctl.at[h]) for h in halves]
    pairs += [(cen_hbm.at[e, :, lanes_of[h]], cen.at[e, h]) for e in range(2) for h in halves]
    fields = len(pairs)
    pairs += [(ens_hbm, ens)] + [(spr_hbm.at[:, lanes_of[h]], spr.at[h]) for h in halves]
    small = len(pairs)
    pairs += [(jac_hbm.at[pl.ds(my_lev * (slots // levs), slots // levs)], jac.at[my_lev]), (val_hbm, val_ref), (wgt_hbm, wgt_ref), (msk_hbm, msk_ref), (count_hbm, count_ref)]
    pairs += [(cell_hbm, cell_ref)]
    loads = [pltpu.make_async_copy(src, dst, in_sem.at[i]) for i, (src, dst) in enumerate(pairs)]
    loads[-1].start()
    barrier = pltpu.get_barrier_semaphore()
    peers = cols * levs
    my_id = me * levs + my_lev
    for axis, count, mine in (("col", cols, me), ("lev", levs, my_lev)):
        for d in range(1, count):
            pl.semaphore_signal(
                barrier, inc=1, device_id={axis: lax.rem(mine + d, count)}, device_id_type=pl.DeviceIdType.MESH
            )
    for load in loads[:-1]:
        load.start()

    def send(phase, axis, src_of, dst):
        count, mine = {"col": (cols, me), "lev": (levs, my_lev), "all": (peers, my_id)}[axis]
        copies = []
        for d in range(1, count):
            to = lax.rem(mine + d, count)
            device = {"col": lax.div(to, levs), "lev": lax.rem(to, levs)} if axis == "all" else {axis: to}
            copy = pltpu.make_async_remote_copy(
                src_ref=src_of(to),
                dst_ref=dst,
                send_sem=send_sem.at[phase, d],
                recv_sem=recv_sem.at[phase, d],
                device_id=device,
                device_id_type=pl.DeviceIdType.MESH,
            )
            copy.start()
            copies.append(copy)
        return copies

    loads[-1].wait()
    pack = slots // 2
    row = lax.broadcasted_iota(jnp.int32, (pack, LANES), 0)
    first = lax.broadcasted_iota(jnp.int32, (pack, LANES), 1) < LANES // 2
    own = jnp.zeros((pack, LANES), jnp.int32)
    for r in range(pack):
        own = jnp.where(row == r, jnp.where(first, cell_ref[r], cell_ref[pack + r]), own)
    my_rows = pl.ds(pl.multiple_of(me * pack, pack), pack)
    cells[my_rows, :] = own
    pl.semaphore_wait(barrier, cols + levs - 2)
    cell_copies = send(0, "col", lambda to: cells.at[my_rows], cells.at[my_rows])
    share = slots // levs
    jac_copies = send(2, "lev", lambda to: jac_hbm.at[pl.ds(to * share, share)], jac.at[my_lev])

    for load in loads[:fields]:
        load.wait()
    zeros = jnp.zeros((lev, ny), jnp.bfloat16)
    picks = [pl.ds(x, lev, stride=cx) for x in range(cx)]
    for x in range(cx):
        for i, ref in enumerate((ctl, cen.at[0], cen.at[1])):
            for h in halves:
                high, low = split(ref.at[h][picks[x], :])
                fst[x, i * lev : (i + 1) * lev, lanes_of[h]] = high
                fst[x, LANES + i * lev : LANES + (i + 1) * lev, lanes_of[h]] = low
        fst[x, 3 * lev : 4 * lev, :] = zeros
        fst[x, LANES + 3 * lev : LANES + 4 * lev, :] = zeros
    for load in loads[fields:small]:
        load.wait()
    for e in range(2):
        member = ens[e].astype(jnp.float32).reshape(lev * cx, ny)
        for h in halves:
            ensf[e, h] = member[:, lanes_of[h]]
    for x in range(cx):
        for h in halves:
            high, low = split(spr.at[h][picks[x], :])
            vst[x, 0:lev, lanes_of[h]] = high
            vst[x, lev : 2 * lev, lanes_of[h]] = ensf.at[0, h][picks[x], :].astype(jnp.bfloat16)
            vst[x, 2 * lev : 3 * lev, lanes_of[h]] = ensf.at[1, h][picks[x], :].astype(jnp.bfloat16)
            vst[x, 3 * lev : 4 * lev, lanes_of[h]] = low

    for copy in cell_copies:
        copy.wait()

    rows_of = []
    for s in range(cols):
        packed = cells[s * pack : (s + 1) * pack, :]
        turned = pltpu.roll(packed, LANES // 2, 1)
        rows_of += [jnp.where(first, packed, turned), jnp.where(first, turned, packed)]
    cell = jnp.concatenate(rows_of, axis=0)
    shift = ny.bit_length() - 1
    cell_x = lax.shift_right_logical(cell, jnp.full_like(cell, shift))
    cell_y = cell & (ny - 1)
    slot = lax.broadcasted_iota(jnp.int32, (every, LANES), 0)
    target = lax.shift_right_logical(slot, jnp.full_like(slot, cap.bit_length() - 1)) & (cols - 1)
    apart = me * cx - (target * cx + cell_x)
    y_lane = lax.broadcasted_iota(jnp.int32, (every, LANES), 1)
    for h in range(ny // LANES):
        y = y_lane + h * LANES
        dy = jnp.abs(y - cell_y)
        below = y + cell_y + 2
        above = 2 * ny - y - cell_y
        for m in range(STEPS + 1):
            one = jnp.where(dy == m, 1.0, 0.0)
            if m >= 2:
                one = one - jnp.where((below == m) | (above == m), 1.0, 0.0)
            ey[m, :, h * LANES : (h + 1) * LANES] = one
    out = None
    for x in range(cx):
        dx = apart + x
        dx = jnp.where(dx >= nx // 2, dx - nx, dx)
        dx = jnp.abs(jnp.where(dx < -(nx // 2), dx + nx, dx))
        at = [dx == q for q in range(STEPS + 1)]
        factors = []
        for m in range(STEPS + 1):
            factor = jnp.zeros((every, LANES), jnp.float32)
            for q in range(STEPS + 1 - m):
                factor = jnp.where(at[q], float(table[q, m]), factor)
            factors.append(factor)
        here = jnp.where(at[0], 1.0, 0.0)
        hits = []
        for h in range(ny // LANES):
            part = slice(h * LANES, (h + 1) * LANES)
            centre = ey[0, :, part]
            weight = factors[0] * centre
            for m in range(1, STEPS + 1):
                weight = weight + factors[m] * ey[m, :, part]
            high, low = split(weight)
            wst[x, 0:every, part] = high
            wst[x, every : 2 * every, part] = low
            wst[x, 2 * every : 3 * every, part] = high
            hits.append((here * centre).astype(jnp.bfloat16))
        sums = dot(wst[x, 0 : 2 * every, :], fst[x], 1)
        found = dot(jnp.concatenate(hits, axis=1), vst[x], 1)
        out = (sums, found) if out is None else (out[0] + sums, out[1] + found)
    sums, found = out
    wst_store = pltpu.make_async_copy(wst, wst_hbm, out_sem.at[0])
    wst_store.start()
    sums = sums[0:every, 0:LANES] + sums[0:every, LANES:] + sums[every:, 0:LANES]
    group = lax.shift_right_logical(y_lane, jnp.full_like(y_lane, lev.bit_length() - 1))
    found = jnp.where(group == 0, found + pltpu.roll(found, lev, 1), found * (1.0 / math.sqrt(2)))
    found = jnp.where(group == 3, 0.0, found)
    for q in range(peers):
        pv[q, 0:share, :] = sums[q * share : (q + 1) * share]
        pv[q, share:, :] = found[q * share : (q + 1) * share]
    pv_in[my_id] = pv[my_id]
    copies = send(1, "all", lambda to: pv.at[to], pv_in.at[my_id])
    for load in loads[small:-1]:
        load.wait()
    for copy in jac_copies + copies:
        copy.wait()

    row = lax.broadcasted_iota(jnp.int32, (2 * share, LANES), 0)
    lane = lax.broadcasted_iota(jnp.int32, (2 * share, LANES), 1)
    own_lane = lax.shift_right_logical(lane, jnp.full_like(lane, lev.bit_length() - 1)) == (row & (share - 1))
    values, blocks = [], []
    for j in range(levs):
        both = pv_in[j]
        for s in range(1, cols):
            both = both + pv_in[s * levs + j]
        turned = pltpu.roll(both, share, 0)
        values.append(jnp.where(row < share, turned, both))
        blocks.append(jnp.where(own_lane, spread_groups(both * turned, lev), 0.0))
    jac_rows = jac[...].reshape(slots * lev, LANES)
    block = jnp.concatenate([jnp.concatenate(blocks, axis=1)] * 2, axis=0).astype(jnp.bfloat16)
    radiance = dot(block, jac_rows, 0)[0 : 2 * share]

    slot_in = my_lev * share + (row & (share - 1))
    filled = jnp.zeros((2 * share, LANES), jnp.bool_)
    for t in range(cols):
        filled = filled | ((slot_in >= t * cap) & (slot_in < t * cap + jnp.minimum(count_ref[0, t], cap)))

    def mine(ref):
        whole = ref[...].astype(jnp.float32)
        part = whole[0:share]
        for j in range(1, levs):
            part = jnp.where(my_lev == j, whole[j * share : (j + 1) * share], part)
        return jnp.concatenate([part, part], axis=0)

    departure = jnp.where(
        filled & (mine(msk_ref) > 0.0), mine(wgt_ref) * (radiance - mine(val_ref)), 0.0
    )
    dep_in[my_lev] = departure
    dep_copies = send(4, "lev", lambda to: dep_in.at[my_lev], dep_in.at[my_lev])
    doubled = jnp.concatenate([departure, departure], axis=0).astype(jnp.bfloat16)
    spread_out = dot(doubled, jac_rows, 1)[0 : 2 * share]
    half = (row >= share) == ((my_lev & 1) == 1)
    for j in range(levs):
        part = jnp.where(own_lane, spread_out[:, j * LANES : (j + 1) * LANES], 0.0)
        amount = spread_groups(part, lev) * values[j]
        a_out[j] = jnp.where(half, amount, 0.0)
    a_in[my_id] = a_out[my_lev]
    a_copies = send(3, "all", lambda to: a_out.at[lax.rem(to, levs)], a_in.at[my_id])
    for copy in dep_copies:
        copy.wait()
    for j in range(levs):
        dep_ref[j * share : (j + 1) * share, :] = dep_in[j, 0:share, :]
    dep_store = pltpu.make_async_copy(dep_ref, dep_hbm, out_sem.at[out_sem.shape[0] - 1])
    dep_store.start()
    for copy in a_copies:
        copy.wait()
    for q in range(peers // 2):
        a_all[q * 2 * share : (q + 1) * 2 * share, :] = a_in[2 * q] + a_in[2 * q + 1]
    a_store = pltpu.make_async_copy(a_all, a_hbm, out_sem.at[1])
    a_store.start()
    for store in (wst_store, a_store, dep_store):
        store.wait()


def adjoint(
    cfg, ctl_hbm, cen_hbm, wst_hbm, a_hbm, dep_hbm, octl_hbm, ocen_hbm, odep_hbm,
    ctl, cen, wst, amount, dep, in_sem, out_sem,
):
    lev, cx, ny = cfg
    halves = range(ny // LANES)
    lanes_of = [slice(h * LANES, (h + 1) * LANES) for h in halves]
    pairs = [(a_hbm, amount), (wst_hbm, wst)]
    for h in halves:
        pairs += [(ctl_hbm.at[:, lanes_of[h]], ctl.at[h])]
        pairs += [(cen_hbm.at[e, :, lanes_of[h]], cen.at[e, h]) for e in range(2)]
    pairs += [(dep_hbm, dep)]
    loads = [pltpu.make_async_copy(src, dst, in_sem.at[i]) for i, (src, dst) in enumerate(pairs)]
    for load in loads:
        load.start()
    loads[0].wait()
    every = amount.shape[0]
    a_high, a_low = split(amount[...])
    a_high, a_low = a_high.astype(jnp.float32), a_low.astype(jnp.float32)
    left = jnp.concatenate([a_high, a_high, a_low, jnp.zeros_like(a_low)], axis=0).T
    left = left[:, 0 : 3 * every].astype(jnp.bfloat16)
    loads[1].wait()
    stores = []
    for h in halves:
        for load in loads[2 + 3 * h : 5 + 3 * h]:
            load.wait()
        for x in range(cx):
            pick = pl.ds(x, lev, stride=cx)
            add = dot(left, wst[x, :, lanes_of[h]], 0)
            for i, ref in enumerate((ctl.at[h], cen.at[0, h], cen.at[1, h])):
                ref[pick, :] = ref[pick, :] + add[i * lev : (i + 1) * lev]
        pairs = [(ctl.at[h], octl_hbm.at[:, lanes_of[h]])]
        pairs += [(cen.at[e, h], ocen_hbm.at[e, :, lanes_of[h]]) for e in range(2)]
        for src, dst in pairs:
            stores.append(pltpu.make_async_copy(src, dst, out_sem.at[len(stores)]))
            stores[-1].start()
    loads[-1].wait()
    stores.append(pltpu.make_async_copy(dep, odep_hbm, out_sem.at[len(stores)]))
    stores[-1].start()
    for store in stores:
        store.wait()


def fits(members, levels, cells_x, cells_y, slot_total, channels, peers, level_blocks):
    def power(n):
        return n & (n - 1) == 0
    return (
        members == 2 and levels * 4 == LANES and channels == LANES and cells_x == 8
        and cells_y % LANES == 0 and power(cells_y) and cells_y <= 256 and power(peers) and slot_total % 16 == 0
        and power(slot_total // peers) and peers * slot_total * 3 <= 256
        and peers * cells_x > 2 * STEPS and slot_total == 4 * level_blocks and level_blocks == 4
    )


def local_fused(control, control_ens, ensemble, spread, jacobian, obs_value, obs_weight, channel_mask, obs_cell, obs_count):
    members = control_ens.shape[0]
    levels, cells_x, cells_y = control.shape
    slots, _, channels = jacobian.shape
    cols, levs = lax.axis_size("col"), lax.axis_size("lev")
    every, peers, share = cols * slots, cols * levs, slots // levs
    flat = (levels * cells_x, cells_y)
    cut = (cells_y // LANES, levels * cells_x, LANES)
    hbm = pl.BlockSpec(memory_space=pltpu.HBM)
    weights, amount, held = pl.pallas_call(
        functools.partial(fused, (cols, levs, slots, levels, cells_x, cells_y)),
        out_shape=(
            jax.ShapeDtypeStruct((cells_x, 3 * every, cells_y), jnp.bfloat16),
            jax.ShapeDtypeStruct((every, LANES), jnp.float32),
            jax.ShapeDtypeStruct((slots, channels), jnp.float32),
        ),
        in_specs=[hbm] * 10,
        out_specs=(hbm, hbm, hbm),
        scratch_shapes=[
            pltpu.VMEM(cut, jnp.float32),
            pltpu.VMEM((members,) + cut, jnp.float32),
            pltpu.VMEM(ensemble.shape, jnp.bfloat16),
            pltpu.VMEM((members,) + cut, jnp.float32),
            pltpu.VMEM(cut, jnp.float32),
            pltpu.VMEM((levs, share) + jacobian.shape[1:], jnp.bfloat16),
            pltpu.VMEM(obs_value.shape, jnp.bfloat16),
            pltpu.VMEM(obs_weight.shape, jnp.bfloat16),
            pltpu.VMEM(channel_mask.shape, jnp.int32),
            pltpu.SMEM(obs_cell.shape, jnp.int32),
            pltpu.SMEM(obs_count.shape, jnp.int32),
            pltpu.VMEM((every // 2, LANES), jnp.int32),
            pltpu.VMEM((slots, channels), jnp.float32),
            pltpu.VMEM((STEPS + 1, every, cells_y), jnp.float32),
            pltpu.VMEM((cells_x, 2 * LANES, cells_y), jnp.bfloat16),
            pltpu.VMEM((cells_x, LANES, cells_y), jnp.bfloat16),
            pltpu.VMEM((cells_x, 3 * every, cells_y), jnp.bfloat16),
            pltpu.VMEM((peers, 2 * share, LANES), jnp.float32),
            pltpu.VMEM((peers, 2 * share, LANES), jnp.float32),
            pltpu.VMEM((levs, 2 * share, LANES), jnp.float32),
            pltpu.VMEM((levs, 2 * share, LANES), jnp.float32),
            pltpu.VMEM((peers, 2 * share, LANES), jnp.float32),
            pltpu.VMEM((every, LANES), jnp.float32),
            pltpu.SemaphoreType.DMA((7 + (members + 2) * cut[0],)),
            pltpu.SemaphoreType.DMA((3,)),
            pltpu.SemaphoreType.DMA((5, peers)),
            pltpu.SemaphoreType.DMA((5, peers)),
        ],
        compiler_params=pltpu.CompilerParams(
            collective_id=0, has_side_effects=True, vmem_limit_bytes=63 * 1024 * 1024
        ),
    )(
        control.reshape(flat), control_ens.reshape((members,) + flat), ensemble, spread.reshape(flat),
        jacobian, obs_value, obs_weight, channel_mask, obs_cell, obs_count,
    )
    out_control, out_ens, departures = pl.pallas_call(
        functools.partial(adjoint, (levels, cells_x, cells_y)),
        out_shape=(
            jax.ShapeDtypeStruct(flat, jnp.float32),
            jax.ShapeDtypeStruct((members,) + flat, jnp.float32),
            jax.ShapeDtypeStruct((slots, channels), jnp.float32),
        ),
        in_specs=[hbm] * 5,
        out_specs=(hbm,) * 3,
        scratch_shapes=[
            pltpu.VMEM(cut, jnp.float32),
            pltpu.VMEM((members,) + cut, jnp.float32),
            pltpu.VMEM((cells_x, 3 * every, cells_y), jnp.bfloat16),
            pltpu.VMEM((every, LANES), jnp.float32),
            pltpu.VMEM((slots, channels), jnp.float32),
            pltpu.SemaphoreType.DMA((3 + (members + 1) * cut[0],)),
            pltpu.SemaphoreType.DMA((1 + (members + 1) * cut[0],)),
        ],
        compiler_params=pltpu.CompilerParams(vmem_limit_bytes=63 * 1024 * 1024),
    )(control.reshape(flat), control_ens.reshape((members,) + flat), weights, amount, held)
    return out_control.reshape(control.shape), out_ens.reshape(control_ens.shape), departures


def pick_local(control, control_ens, ensemble, spread, jacobian, *obs):
    sizes = (control_ens.shape[0],) + control.shape + (jacobian.shape[0], jacobian.shape[2], lax.axis_size("col"), lax.axis_size("lev"))
    run = local_fused if fits(*sizes) else local
    return run(control, control_ens, ensemble, spread, jacobian, *obs)


def solution(mesh):
    placed = (
        P(("grp", "lev"), "col", None),
        P("grp", "lev", "col", None),
        P("grp", "lev", "col", None),
        P(("grp", "lev"), "col", None),
        P(("grp", "col"), "lev", None),
        P(("grp", "col"), None),
        P(("grp", "col"), None),
        P(("grp", "col"), None),
        P(("grp", "col")),
        P(("grp", "col"), None),
    )
    return jax.shard_map(
        pick_local,
        mesh=mesh,
        in_specs=placed,
        out_specs=(
            P(("grp", "lev"), "col", None),
            P("grp", "lev", "col", None),
            P(("grp", "col"), None),
        ),
        check_vma=False,
    )
```
